512 devices in a mesh: gx: 16 (over x, y_hi, core), gy: 32 (over y_lo, z).
Axes of the slice: x: 4, y: 4 (y_hi: 2, y_lo: 2; y = y_hi * 2 + y_lo), z: 16, core: 2. Of those that a mesh axis runs over, the one named last changes fastest.
Arguments:
- query: bfloat16 [128, 3584], P('gy', 'gx'), may hold values from -48 to 48
- prefix_keys: bfloat16 [262144, 512], P(('gx', 'gy')), may hold values from -16 to 16
- prefix_values: bfloat16 [262144, 512], P(('gx', 'gy')), may hold values from -6 to 6
- suffix_keys: bfloat16 [128, 256, 512], P('gy', 'gx'), may hold values from -9 to 9
- suffix_values: bfloat16 [128, 256, 512], P('gy', 'gx'), may hold values from -6 to 6
- suffix_lengths: int32 [128], P('gy'), may hold values from 1 to 256, as said below
- out_weight: bfloat16 [3584, 3584], P('gx'), may hold values from -0.09375 to 0.09375
Outputs:
- attended: bfloat16 [128, 3584], P('gy', 'gx')
The draws below stay inside these ranges and needn't reach their ends.
Inputs may be any that keep to these rules, and one draw needn't show every extreme that they name: `suffix_lengths`: some sample has exactly 256 live slots.
All inputs are finite; a program needn't handle non-finite values.
Results may differ from the reference program's by a relative error of at most 0.0051.
Values may be sent and summed in bfloat16 or wider, within the bound.
A program may use at most 64 MiB of HBM per device.

```python
import math
import jax
import jax.numpy as jnp
from jax import lax

D = 3584
HQ = 28
KVH = 4
HD = 128
SAMPLES = 128
PREFIX = 262144
SUF = 256


def draw_query(key, part):
    key = jax.random.fold_in(key, 3)
    drawn = jnp.clip(3.0 * jax.random.normal(key, (SAMPLES, HQ * HD), jnp.float32), -48.0, 48.0)
    return drawn.astype(jnp.bfloat16)


def draw_prefix_keys(key, part):
    key = jax.random.fold_in(key, 4)
    drawn = jnp.clip(jax.random.normal(key, (PREFIX, KVH * HD), jnp.float32), -16.0, 16.0)
    return drawn.astype(jnp.bfloat16)


def draw_suffix_lengths(key, part):
    key = jax.random.fold_in(key, 5)
    lengths = jax.random.randint(key, (SAMPLES,), 1, SUF + 1, jnp.int32)
    chosen = jax.random.randint(jax.random.fold_in(key, 6), (), 0, SAMPLES, jnp.int32)
    return lengths.at[chosen].set(SUF)


def levels(key, extent, split, smallest, top_value):
    factor_of, own = 1.0, jax.random.fold_in(key, 6)
    for axis_at, parts in split:
        heights = jnp.exp(jax.random.uniform(jax.random.fold_in(own, axis_at), (parts,), jnp.float32, smallest / len(split), top_value / len(split)))
        factor_of = factor_of * jnp.repeat(heights, extent[axis_at] // parts).reshape([-1 if axis == axis_at else 1 for axis in range(len(extent))])
    return factor_of


def bell_draw(rng, extent, scale, most, shards=(), kind=jnp.bfloat16):
    array = jax.random.normal(rng, extent, jnp.float32) * scale
    if len(shards) > 0:
        array = levels(rng, extent, shards, -0.22, 0.18) * array
    return jnp.clip(array, min=-most, max=most).astype(kind)


def setup_inputs(seed: int = 0) -> dict:
    streams_of = jax.random.split(jax.random.key(seed), 8)
    query = draw_query(jax.random.fold_in(streams_of[7], 71), 0)
    prefix_keys = draw_prefix_keys(jax.random.fold_in(streams_of[7], 71), 0)
    prefix_values = bell_draw(streams_of[2], (PREFIX, KVH * HD), 1.0, 6.0, ((0, 512),))
    suffix_keys = bell_draw(streams_of[3], (SAMPLES, SUF, KVH * HD), 1.5, 9.0, ((0, 32), (1, 16)))
    suffix_values = bell_draw(streams_of[4], (SAMPLES, SUF, KVH * HD), 1.0, 6.0, ((0, 32), (1, 16)))
    suffix_lengths = draw_suffix_lengths(jax.random.fold_in(streams_of[7], 71), 0)
    out_weight = bell_draw(streams_of[6], (HQ * HD, D), (HQ * HD) ** -0.5, 0.09375, ((0, 16),))
    return dict(query=query, prefix_keys=prefix_keys, prefix_values=prefix_values, suffix_keys=suffix_keys, suffix_values=suffix_values, suffix_lengths=suffix_lengths, out_weight=out_weight)


def reference(query, prefix_keys, prefix_values, suffix_keys, suffix_values, suffix_lengths, out_weight):
    group = HQ // KVH
    scale = 1.0 / math.sqrt(HD)
    total = prefix_keys.shape[0]
    block = min(4096, total)
    count = total // block
    rows = SAMPLES * group
    queries = [query[:, g * group * HD:(g + 1) * group * HD].reshape(rows, HD) for g in range(KVH)]
    dims = (((1,), (1,)), ((), ()))

    def scores_at(index, g):
        keys = lax.dynamic_slice_in_dim(prefix_keys, index * block, block, 0)[:, g * HD:(g + 1) * HD]
        return lax.dot_general(queries[g], keys, dims, preferred_element_type=jnp.float32) * scale

    def max_step(carry, index):
        found = jnp.stack([lax.optimization_barrier(jnp.max(scores_at(index, g), axis=1)) for g in range(KVH)])
        return (jnp.maximum(carry, found), None)
    start = jnp.full((KVH, rows), -1e+30, jnp.float32)
    prefix_max, _ = lax.scan(max_step, start, jnp.arange(count, dtype=jnp.int32))
    query_four = query.reshape(SAMPLES, KVH, group, HD).astype(jnp.float32)
    keys_four = suffix_keys.reshape(SAMPLES, SUF, KVH, HD).astype(jnp.float32)
    values_four = suffix_values.reshape(SAMPLES, SUF, KVH, HD).astype(jnp.float32)
    suffix_scores = jnp.einsum('sghd,stgd->sght', query_four, keys_four) * scale
    positions = jnp.arange(SUF, dtype=jnp.int32)
    valid = (positions[None, :] < suffix_lengths[:, None])[:, None, None, :]
    masked = jnp.where(valid, suffix_scores, jnp.float32(-1e+30))
    suffix_max = lax.optimization_barrier(jnp.max(masked, axis=-1))
    top = jnp.maximum(prefix_max.reshape(KVH, SAMPLES, group).transpose(1, 0, 2), suffix_max)
    top_rows = top.transpose(1, 0, 2).reshape(KVH, rows)

    def sum_step(carry, index):
        numer, denom = carry
        values = lax.dynamic_slice_in_dim(prefix_values, index * block, block, 0)
        new_numer = []
        new_denom = []
        for g in range(KVH):
            probs = jnp.exp(scores_at(index, g) - top_rows[g][:, None])
            new_denom.append(denom[g] + lax.optimization_barrier(jnp.sum(probs, axis=1)))
            new_numer.append(numer[g] + jnp.dot(probs.astype(jnp.bfloat16), values[:, g * HD:(g + 1) * HD], preferred_element_type=jnp.float32))
        return ((jnp.stack(new_numer), jnp.stack(new_denom)), None)
    zeros = (jnp.zeros((KVH, rows, HD), jnp.float32), jnp.zeros((KVH, rows), jnp.float32))
    (numer, denom), _ = lax.scan(sum_step, zeros, jnp.arange(count, dtype=jnp.int32))
    numer = numer.reshape(KVH, SAMPLES, group, HD).transpose(1, 0, 2, 3)
    denom = denom.reshape(KVH, SAMPLES, group).transpose(1, 0, 2)
    suffix_probs = jnp.where(valid, jnp.exp(masked - top[..., None]), jnp.float32(0.0))
    denom = denom + lax.optimization_barrier(jnp.sum(suffix_probs, axis=-1))
    rounded = lax.optimization_barrier(suffix_probs.astype(jnp.bfloat16)).astype(jnp.float32)
    numer = numer + jnp.einsum('sght,stgd->sghd', rounded, values_four)
    heads = (numer / denom[..., None]).astype(jnp.bfloat16).reshape(SAMPLES, HQ * HD)
    return jnp.dot(heads, out_weight, preferred_element_type=jnp.float32).astype(jnp.bfloat16)
```

```python
import math

import jax
import jax.numpy as jnp
from jax import lax
from jax.experimental import pallas as pl
from jax.experimental.pallas import tpu as pltpu
from jax.sharding import PartitionSpec as P

MESH = pl.DeviceIdType.MESH
F32, BF16 = jnp.float32, jnp.bfloat16
HD = 128
SCALE = math.log2(math.e) / math.sqrt(HD)
ROW_DIMS = (((1,), (1,)), ((), ()))


def iota(shape, axis):
    return lax.broadcasted_iota(jnp.int32, shape, axis)


def with_stats(values, top, total, split):
    lane, row = iota((1, 8, 128), 2), iota((1, 8, 128), 1)
    if split:
        high = total.astype(BF16).astype(F32)
        low = jnp.where(lane == row + 16, total - high, 0.0)
        total = high
    else:
        low = 0.0
    stats = jnp.where(lane == row, total, 0.0) + jnp.where(lane == row + 8, top, 0.0) + low
    return jnp.where(row == 7, jnp.sum(stats, axis=1, keepdims=True), values)


def read_stats(tiles, split):
    lane, row = iota((1, 8, 128), 2), iota((1, 8, 128), 1)
    last = tiles[:, 7:8, :]
    here = lane == row
    if split:
        here = here | (lane == row + 16)
    total = jnp.sum(jnp.where(here, last, 0.0), axis=2, keepdims=True)
    top = jnp.sum(jnp.where(lane == row + 8, last, 0.0), axis=2, keepdims=True)
    return top, total


def merge(parts):
    top = parts[0][1]
    for part in parts[1:]:
        top = jnp.maximum(top, part[1])
    values, total = 0.0, 0.0
    for part_values, part_top, part_total in parts:
        weight = jnp.exp2(part_top - top)
        values = values + weight * part_values
        total = total + weight * part_total
    return values, top, total


def kernel(
    q_ref, k_hbm, v_hbm, sk_hbm, sv_hbm, len_ref, w_hbm, o_ref,
    kbuf, vbuf, wraw, wp, sbuf, sfx, ztile, qsend, qall, xf, qf, s_ref,
    osend, orecv, zsend, zrecv, hbuf, psend, precv,
    local_sem, k_ss, k_rs, v_ss, v_rs, s_ss, s_rs, r_ss, r_rs, l_ss, l_rs,
    qa_ss, qa_rs, o_ss, o_rs, z_ss, z_rs, h_ss, h_rs, p_ss, p_rs,
):
    gx, gy = lax.axis_index("gx"), lax.axis_index("gy")
    x, yh, c = gx // 4, (gx // 2) % 2, gx % 2
    yl, z = gy // 16, gy % 16
    y = 2 * yh + yl

    def dev(x_=None, y_=None, c_=None, z_=None):
        x_ = x if x_ is None else x_
        y_ = y if y_ is None else y_
        c_ = c if c_ is None else c_
        z_ = z if z_ is None else z_
        return (x_ * 4 + (y_ // 2) * 2 + c_, (y_ % 2) * 16 + z_)

    def lanes(i):
        return pl.ds(pl.multiple_of(i * HD, HD), HD)

    sent = []

    def send(src, dst, ss, rs, to):
        copy = pltpu.make_async_remote_copy(
            src_ref=src, dst_ref=dst, send_sem=ss, recv_sem=rs, device_id=to, device_id_type=MESH
        )
        copy.start()
        sent.append(copy)

    def arrived(dst, rs):
        pltpu.make_async_remote_copy(
            src_ref=dst, dst_ref=dst, send_sem=rs, recv_sem=rs, device_id=dev(z_=(z + 1) % 16),
            device_id_type=MESH,
        ).wait_recv()

    around = [dev(z_=(z + 1) % 16), dev(z_=(z + 15) % 16)]
    around += [dev(x_=(x + d) % 4) for d in (1, 2, 3)]
    partners = [(dy, dc) for dy in (2, 1, 3, 0) for dc in (0, 1) if dy or dc]
    around += [dev(y_=(y + dy) % 4, c_=(c + dc) % 2) for dy, dc in partners]
    barrier = pltpu.get_barrier_semaphore()
    for to in around:
        pl.semaphore_signal(barrier, inc=1, device_id=to, device_id_type=MESH)

    local = [
        pltpu.make_async_copy(k_hbm.at[:, lanes(x)], kbuf.at[0], local_sem.at[0]),
        pltpu.make_async_copy(v_hbm.at[:, lanes(x)], vbuf.at[0], local_sem.at[1]),
        pltpu.make_async_copy(w_hbm, wraw, local_sem.at[2]),
    ]
    for g in range(4):
        for at, ref in enumerate((sk_hbm, sv_hbm)):
            local.append(
                pltpu.make_async_copy(
                    ref.at[:, :, g * HD : (g + 1) * HD], sbuf.at[g, :, at], local_sem.at[3 + 2 * g + at]
                )
            )
    for copy in local:
        copy.start()
    query = q_ref[...].astype(F32)
    ztile[8] = jnp.zeros((8, 128), F32)
    ztile[8, pl.ds(0, 4, stride=2), :] = query[:, 0:128]
    ztile[8, pl.ds(1, 4, stride=2), 0:96] = query[:, 128:224]

    pl.semaphore_wait(barrier, len(around))

    for d in (2, 1, 3):
        to = (x + d) % 4
        send(k_hbm.at[:, lanes(to)], kbuf.at[d], k_ss.at[d], k_rs.at[d], dev(x_=to))
    for d in (2, 1, 3):
        to = (x + d) % 4
        send(v_hbm.at[:, lanes(to)], vbuf.at[d], v_ss.at[d], v_rs.at[d], dev(x_=to))

    mine = yl * 4 + 2 * yh + c

    def to_partners(piece, first, count):
        rows = pl.ds(first * 8, count * 8)
        packed = ztile[first : first + count].reshape(count * 8, 128).astype(BF16)
        qall[mine, rows, :] = packed
        qsend[rows, :] = packed
        for at, (dy, dc) in enumerate(partners):
            send(
                qsend.at[rows], qall.at[mine, rows], qa_ss.at[piece, at], qa_rs.at[piece, mine],
                dev(y_=(y + dy) % 4, c_=(c + dc) % 2),
            )

    for s in range(8):
        if s:
            arrived(ztile.at[8 - s], r_rs.at[8 - s])
        send(ztile.at[8 - s], ztile.at[7 - s], r_ss.at[s], r_rs.at[7 - s], dev(z_=(z + 1) % 16))
        if s:
            arrived(ztile.at[8 + s], l_rs.at[8 + s])
        if s < 7:
            send(ztile.at[8 + s], ztile.at[9 + s], l_ss.at[s], l_rs.at[9 + s], dev(z_=(z + 15) % 16))
        if s == 4:
            to_partners(0, 4, 8)
    to_partners(1, 12, 4)
    arrived(ztile.at[0], r_rs.at[0])
    to_partners(2, 0, 4)

    local[2].wait()
    wp[:, 224:256, :] = jnp.zeros((16, 32, 256), BF16)
    lane = iota((224, 128), 1)

    def relay(q, carry):
        for r in range(4):
            first, off = (224 * r) // 128, (224 * r) % 128
            tiles = []
            for n in range(3):
                if n < 2 or off >= 64:
                    at = pl.multiple_of(q * 896 + (first + n) * 128, 128)
                    tile = wraw[:, pl.ds(at, 128)].astype(F32)
                    tiles.append(pltpu.roll(tile, 128 - off, 1) if off else tile)
                else:
                    tiles.append(jnp.zeros((224, 128), F32))
            for n in range(2):
                block = jnp.where(lane < 128 - off, tiles[n], tiles[n + 1])
                wp[q * 4 + r, 0:224, n * 128 : (n + 1) * 128] = block.astype(BF16)
        return carry

    lax.fori_loop(0, 4, relay, 0)

    for dy, dc in partners:
        source = (y + dy) % 4
        source = (source % 2) * 4 + (source // 2) * 2 + (c + dc) % 2
        for piece, (first, count) in enumerate(((4, 8), (12, 4), (0, 4))):
            arrived(qall.at[source, pl.ds(first * 8, count * 8)], qa_rs.at[piece, source])
    lane = iota((16, 128), 1)
    xf[...] = qall[...].astype(F32)
    qf[...] = jnp.zeros_like(qf)
    for at in range(8):
        t = at % 4
        pieces = []
        for b in range(4):
            for half in range(2):
                pieces.append(xf[at // 4 * 4 + b, pl.ds(2 * t + half, 16, stride=8), :])
        starts = [224 * (n // 2) + 128 * (n % 2) for n in range(8)]
        sizes = [128 if n % 2 == 0 else 96 for n in range(8)]
        for h in range(7):
            head = None
            for n in range(8):
                low = max(starts[n], 128 * h)
                high = min(starts[n] + sizes[n], 128 * h + 128)
                if low < high:
                    shift = (starts[n] - 128 * h) % 128
                    moved = pltpu.roll(pieces[n], shift, 1) if shift else pieces[n]
                    if head is None:
                        head = moved
                    else:
                        head = jnp.where(lane < low - 128 * h, head, moved)
            qf[at, pl.ds(h, 16, stride=8), :] = head

    local[0].wait()
    local[1].wait()
    for copy in local[3:]:
        copy.wait()
    for d in (2, 1, 3):
        arrived(kbuf.at[d], k_rs.at[d])
    for d in (2, 1, 3):
        arrived(vbuf.at[d], v_rs.at[d])

    sfx[gx] = sbuf[x, 2 * yh + c]
    for d in range(1, 16):
        to = (gx + d) % 16
        send(sbuf.at[to // 4, to % 4], sfx.at[gx], s_ss.at[d], s_rs.at[gx], (to, gy))

    for dy in (2, 1, 3, 0):
        to_y = (y + dy) % 4
        first = (to_y % 2) * 4 + (to_y // 2) * 2
        rows = qf[pl.ds(first, 2)].reshape(256, 128).astype(BF16)
        top = None
        for n in range(4):
            scores = lax.dot_general(rows, kbuf[n], ROW_DIMS, preferred_element_type=F32)
            s_ref[:, n * 512 : (n + 1) * 512] = scores
            for m in range(4):
                part = scores[:, m * 128 : (m + 1) * 128]
                top = part if top is None else jnp.maximum(top, part)
        top = (jnp.max(top, axis=1, keepdims=True) * SCALE).astype(BF16).astype(F32)
        total, values = 0.0, 0.0
        for n in range(4):
            probs = jnp.exp2(s_ref[:, n * 512 : (n + 1) * 512] * SCALE - top)
            for m in range(4):
                total = total + probs[:, m * 128 : (m + 1) * 128]
            values = values + jnp.dot(probs.astype(BF16), vbuf[n], preferred_element_type=F32)
        total = jnp.sum(total, axis=1, keepdims=True)
        packed = with_stats(
            values.reshape(32, 8, 128), top.reshape(32, 8, 1), total.reshape(32, 8, 1), True
        )
        osend[dy] = packed.reshape(2, 128, 128).astype(BF16)
        if dy:
            for to_c in range(2):
                send(
                    osend.at[dy, to_c], orecv.at[dy * 2 + c], o_ss.at[dy * 2 + to_c], o_rs.at[dy * 2 + c],
                    dev(y_=to_y, c_=to_c),
                )
        else:
            send(osend.at[0, 1 - c], orecv.at[c], o_ss.at[0], o_rs.at[c], dev(c_=1 - c))
            orecv[c] = osend[0, c]

    for d in range(1, 16):
        source = (gx + d) % 16
        arrived(sfx.at[source], s_rs.at[source])
    own = qf[mine, 64:72, :].astype(BF16)
    suffix_keys = sfx[:, 0].reshape(256, 128)
    suffix_values = sfx[:, 1].reshape(256, 128)
    scores = lax.dot_general(own, suffix_keys, ROW_DIMS, preferred_element_type=F32) * SCALE
    live = iota((8, 256), 1) < len_ref[2 * yh + c]
    scores = jnp.where(live, scores, -1e30)
    suffix_top = jnp.max(scores, axis=1, keepdims=True)
    probs = jnp.where(live, jnp.exp2(scores - suffix_top), 0.0)
    suffix_total = jnp.sum(probs, axis=1, keepdims=True)
    suffix_out = jnp.dot(probs.astype(BF16), suffix_values, preferred_element_type=F32)

    for dy in (2, 1, 3):
        for from_c in range(2):
            arrived(orecv.at[dy * 2 + from_c], o_rs.at[dy * 2 + from_c])
    arrived(orecv.at[1 - c], o_rs.at[1 - c])
    parts = []
    for n in range(8):
        tiles = orecv[n].astype(F32).reshape(16, 8, 128)
        parts.append((tiles,) + read_stats(tiles, True))
    zsend[...] = with_stats(*merge(parts), False)

    for p in (0, 1, 15, 2, 14, 3, 13, 4, 12, 5, 11, 6, 10, 7, 9):
        send(zsend.at[p], zrecv.at[p], z_ss.at[p], z_rs.at[p], dev(z_=(z + p + 8) % 16))
    zrecv[8] = zsend[8]
    for p in range(16):
        if p != 8:
            arrived(zrecv.at[p], z_rs.at[p])
    tiles = zrecv[...]
    tops, totals = read_stats(tiles, False)
    parts = [(tiles[p], tops[p], totals[p]) for p in range(16)]
    parts.append((suffix_out, suffix_top, suffix_total))
    values, _, total = merge(parts)
    heads = jnp.where(iota((8, 128), 0) < 7, values / total, 0.0)

    hbuf[2 * yh + c] = heads
    for at, (dyh, dc) in enumerate(((1, 0), (1, 1), (0, 1))):
        to = dev(y_=(y + 2 * dyh) % 4, c_=(c + dc) % 2)
        send(hbuf.at[2 * yh + c], hbuf.at[2 * yh + c], h_ss.at[at], h_rs.at[2 * yh + c], to)
    for dyh, dc in ((1, 0), (1, 1), (0, 1)):
        source = 2 * ((yh + dyh) % 2) + (c + dc) % 2
        arrived(hbuf.at[source], h_rs.at[source])

    feature = 224 * (2 * yh + c)
    head, off = feature // 128, feature % 128
    lane = iota((8, 128), 1)
    moved = []
    for n in range(3):
        four = jnp.concatenate([hbuf[t, pl.ds(head + n, 1), :] for t in range(4)], axis=0)
        eight = jnp.concatenate([four, four], axis=0)
        moved.append(pltpu.roll(eight, (128 - off) % 128, 1))
    left = jnp.where(lane < 128 - off, moved[0], moved[1])
    right = jnp.where(lane < 128 - off, moved[1], moved[2])
    right = jnp.where(lane < 96, right, 0.0)
    features = jnp.concatenate([left, right], axis=1).astype(BF16)
    row = iota((8, 128), 0)
    for d in tuple(range(1, 16)) + (0,):
        to = (gx + d) % 16
        product = jnp.dot(features, wp[to], preferred_element_type=F32)
        tile = jnp.where(row < 4, product[:, 0:128], product[:, 128:256])
        if d:
            psend[d] = tile
            send(psend.at[d], precv.at[d], p_ss.at[d], p_rs.at[d], (to, gy))
        else:
            result = tile
    for d in range(1, 16):
        arrived(precv.at[d], p_rs.at[d])
    for d in range(1, 16):
        result = result + precv[d]
    o_ref[:, 0:128] = result[0:4].astype(BF16)
    o_ref[:, 128:224] = result[4:8, 0:96].astype(BF16)
    for copy in sent:
        copy.wait_send()


def on_device(query, keys, values, suffix_keys, suffix_values, lengths, out_weight):
    vmem = pl.BlockSpec(memory_space=pltpu.VMEM)
    hbm = pl.BlockSpec(memory_space=pl.ANY)
    dma = pltpu.SemaphoreType.DMA
    return pl.pallas_call(
        kernel,
        out_shape=jax.ShapeDtypeStruct((4, 224), BF16),
        in_specs=[vmem, hbm, hbm, hbm, hbm, pl.BlockSpec(memory_space=pltpu.SMEM), hbm],
        out_specs=vmem,
        scratch_shapes=[
            pltpu.VMEM((4, 512, 128), BF16),
            pltpu.VMEM((4, 512, 128), BF16),
            pltpu.VMEM((224, 3584), BF16),
            pltpu.VMEM((16, 256, 256), BF16),
            pltpu.VMEM((4, 4, 2, 16, 128), BF16),
            pltpu.VMEM((16, 2, 16, 128), BF16),
            pltpu.VMEM((16, 8, 128), F32),
            pltpu.VMEM((128, 128), BF16),
            pltpu.VMEM((8, 128, 128), BF16),
            pltpu.VMEM((8, 128, 128), F32),
            pltpu.VMEM((8, 128, 128), F32),
            pltpu.VMEM((256, 2048), F32),
            pltpu.VMEM((4, 2, 128, 128), BF16),
            pltpu.VMEM((8, 128, 128), BF16),
            pltpu.VMEM((16, 8, 128), F32),
            pltpu.VMEM((16, 8, 128), F32),
            pltpu.VMEM((4, 8, 128), F32),
            pltpu.VMEM((16, 8, 128), F32),
            pltpu.VMEM((16, 8, 128), F32),
            dma((11,)),
            dma((4,)), dma((4,)), dma((4,)), dma((4,)),
            dma((16,)), dma((16,)),
            dma((8,)), dma((8,)), dma((8,)), dma((16,)),
            dma((3, 7)), dma((3, 8)),
            dma((8,)), dma((8,)),
            dma((16,)), dma((16,)),
            dma((3,)), dma((4,)),
            dma((16,)), dma((16,)),
        ],
        compiler_params=pltpu.CompilerParams(
            collective_id=0, has_side_effects=True, vmem_limit_bytes=40 * 2**20
        ),
        name="decode_attention",
    )(query, keys, values, suffix_keys, suffix_values, lengths, out_weight)


def solution(mesh):
    return jax.shard_map(
        on_device,
        mesh=mesh,
        in_specs=(
            P("gy", "gx"),
            P(("gx", "gy"), None),
            P(("gx", "gy"), None),
            P("gy", "gx", None),
            P("gy", "gx", None),
            P("gy"),
            P("gx", None),
        ),
        out_specs=P("gy", "gx"),
        check_vma=False,
    )
```

```python
import math

import jax
import jax.numpy as jnp
from jax import lax
from jax.experimental import pallas as pl
from jax.experimental.pallas import tpu as pltpu
from jax.sharding import PartitionSpec as P

MESH = pl.DeviceIdType.MESH
F32, BF16 = jnp.float32, jnp.bfloat16
HD = 128
SCALE = math.log2(math.e) / math.sqrt(HD)
ROW_DIMS = (((1,), (1,)), ((), ()))


def iota(shape, axis):
    return lax.broadcasted_iota(jnp.int32, shape, axis)


def with_stats(values, top, total, split):
    lane, row = iota((1, 8, 128), 2), iota((1, 8, 128), 1)
    if split:
        high = total.astype(BF16).astype(F32)
        low = jnp.where(lane == row + 16, total - high, 0.0)
        total = high
    else:
        low = 0.0
    stats = jnp.where(lane == row, total, 0.0) + jnp.where(lane == row + 8, top, 0.0) + low
    return jnp.where(row == 7, jnp.sum(stats, axis=1, keepdims=True), values)


def read_stats(tiles, split):
    lane, row = iota((1, 8, 128), 2), iota((1, 8, 128), 1)
    last = tiles[:, 7:8, :]
    here = lane == row
    if split:
        here = here | (lane == row + 16)
    total = jnp.sum(jnp.where(here, last, 0.0), axis=2, keepdims=True)
    top = jnp.sum(jnp.where(lane == row + 8, last, 0.0), axis=2, keepdims=True)
    return top, total


def merge(parts):
    top = parts[0][1]
    for part in parts[1:]:
        top = jnp.maximum(top, part[1])
    values, total = 0.0, 0.0
    for part_values, part_top, part_total in parts:
        weight = jnp.exp2(part_top - top)
        values = values + weight * part_values
        total = total + weight * part_total
    return values, top, total


def kernel(
    q_hbm, k_hbm, v_hbm, sk_hbm, sv_hbm, len_hbm, w_hbm, o_ref,
    q_ref, len_ref, kbuf, vbuf, wraw, wp, sbuf, sfx, ztile, qsend, qall, xf, qf, s_ref,
    osend, orecv, zsend, zrecv, hbuf, psend, precv,
    local_sem, k_ss, k_rs, v_ss, v_rs, s_ss, s_rs, r_ss, r_rs,
    qa_ss, qa_rs, o_ss, o_rs, z_ss, z_rs, h_ss, h_rs, p_ss, p_rs,
):
    gx, gy = lax.axis_index("gx"), lax.axis_index("gy")
    x, yh, c = gx // 4, (gx // 2) % 2, gx % 2
    yl, z = gy // 16, gy % 16
    y = 2 * yh + yl

    def dev(x_=None, y_=None, c_=None, z_=None):
        x_ = x if x_ is None else x_
        y_ = y if y_ is None else y_
        c_ = c if c_ is None else c_
        z_ = z if z_ is None else z_
        return (x_ * 4 + (y_ // 2) * 2 + c_, (y_ % 2) * 16 + z_)

    def lanes(i):
        return pl.ds(pl.multiple_of(i * HD, HD), HD)

    sent = []

    def send(src, dst, ss, rs, to):
        copy = pltpu.make_async_remote_copy(
            src_ref=src, dst_ref=dst, send_sem=ss, recv_sem=rs, device_id=to, device_id_type=MESH
        )
        copy.start()
        sent.append(copy)

    def arrived(dst, rs):
        pltpu.make_async_remote_copy(
            src_ref=dst, dst_ref=dst, send_sem=rs, recv_sem=rs, device_id=dev(z_=(z + 1) % 16),
            device_id_type=MESH,
        ).wait_recv()

    around = [dev(z_=(z + hops) % 16) for hops in (1, 2, 3, 4, 12, 13, 14, 15)]
    around += [dev(x_=(x + d) % 4) for d in (1, 2, 3)]
    partners = [(dy, dc) for dy in (2, 1, 3, 0) for dc in (0, 1) if dy or dc]
    around += [dev(y_=(y + dy) % 4, c_=(c + dc) % 2) for dy, dc in partners]
    barrier = pltpu.get_barrier_semaphore()
    for to in around:
        pl.semaphore_signal(barrier, inc=1, device_id=to, device_id_type=MESH)

    local = [
        pltpu.make_async_copy(k_hbm.at[:, lanes(x)], kbuf.at[0], local_sem.at[0]),
        pltpu.make_async_copy(v_hbm.at[:, lanes(x)], vbuf.at[0], local_sem.at[1]),
        pltpu.make_async_copy(w_hbm, wraw, local_sem.at[2]),
    ]
    for g in range(4):
        for at, ref in enumerate((sk_hbm, sv_hbm)):
            local.append(
                pltpu.make_async_copy(
                    ref.at[:, :, g * HD : (g + 1) * HD], sbuf.at[g, :, at], local_sem.at[3 + 2 * g + at]
                )
            )
    local.append(pltpu.make_async_copy(len_hbm, len_ref, local_sem.at[11]))
    fetch = pltpu.make_async_copy(q_hbm, q_ref, local_sem.at[12])
    fetch.start()
    for copy in local:
        copy.start()
    fetch.wait()
    query = q_ref[...].astype(F32)
    ztile[8] = jnp.zeros((8, 128), F32)
    ztile[8, pl.ds(0, 4, stride=2), :] = query[:, 0:128]
    ztile[8, pl.ds(1, 4, stride=2), 0:96] = query[:, 128:224]

    pl.semaphore_wait(barrier, len(around))

    for d in (2, 1, 3):
        to = (x + d) % 4
        send(k_hbm.at[:, lanes(to)], kbuf.at[d], k_ss.at[d], k_rs.at[d], dev(x_=to))
    for d in (2, 1, 3):
        to = (x + d) % 4
        send(v_hbm.at[:, lanes(to)], vbuf.at[d], v_ss.at[d], v_rs.at[d], dev(x_=to))

    mine = yl * 4 + 2 * yh + c

    def to_partners(piece, first, count):
        rows = pl.ds(first * 8, count * 8)
        packed = ztile[first : first + count].reshape(count * 8, 128).astype(BF16)
        qall[mine, rows, :] = packed
        qsend[rows, :] = packed
        for at, (dy, dc) in enumerate(partners):
            send(
                qsend.at[rows], qall.at[mine, rows], qa_ss.at[piece, at], qa_rs.at[piece, mine],
                dev(y_=(y + dy) % 4, c_=(c + dc) % 2),
            )

    def along_z(first, count, to_first, slot, hops):
        send(
            ztile.at[pl.ds(first, count)], ztile.at[pl.ds(to_first, count)], r_ss.at[slot], r_rs.at[slot],
            dev(z_=(z + 16 + hops) % 16),
        )

    def from_z(first, count, slot):
        arrived(ztile.at[pl.ds(first, count)], r_rs.at[slot])

    for hops in (4, 3, 2, 1):
        along_z(8, 1, 8 - hops, 8 - hops, hops)
        along_z(8, 1, 8 + hops, 8 + hops, -hops)
    for p in (7, 6, 5, 4):
        from_z(p, 1, p)
    along_z(4, 4, 0, 0, 4)
    for p in (9, 10, 11):
        from_z(p, 1, p)
    along_z(9, 3, 13, 13, -4)
    to_partners(0, 4, 8)
    from_z(12, 1, 12)
    from_z(13, 3, 13)
    to_partners(1, 12, 4)
    from_z(0, 4, 0)
    to_partners(2, 0, 4)

    local[2].wait()
    wp[:, 224:256, :] = jnp.zeros((16, 32, 256), BF16)
    lane = iota((224, 128), 1)

    def relay(q, carry):
        for r in range(4):
            first, off = (224 * r) // 128, (224 * r) % 128
            tiles = []
            for n in range(3):
                if n < 2 or off >= 64:
                    at = pl.multiple_of(q * 896 + (first + n) * 128, 128)
                    tile = wraw[:, pl.ds(at, 128)].astype(F32)
                    tiles.append(pltpu.roll(tile, 128 - off, 1) if off else tile)
                else:
                    tiles.append(jnp.zeros((224, 128), F32))
            for n in range(2):
                block = jnp.where(lane < 128 - off, tiles[n], tiles[n + 1])
                wp[q * 4 + r, 0:224, n * 128 : (n + 1) * 128] = block.astype(BF16)
        return carry

    lax.fori_loop(0, 4, relay, 0)

    for dy, dc in partners:
        source = (y + dy) % 4
        source = (source % 2) * 4 + (source // 2) * 2 + (c + dc) % 2
        for piece, (first, count) in enumerate(((4, 8), (12, 4), (0, 4))):
            arrived(qall.at[source, pl.ds(first * 8, count * 8)], qa_rs.at[piece, source])
    lane = iota((16, 128), 1)
    xf[...] = qall[...].astype(F32)
    qf[...] = jnp.zeros_like(qf)
    for at in range(8):
        t = at % 4
        pieces = []
        for b in range(4):
            for half in range(2):
                pieces.append(xf[at // 4 * 4 + b, pl.ds(2 * t + half, 16, stride=8), :])
        starts = [224 * (n // 2) + 128 * (n % 2) for n in range(8)]
        sizes = [128 if n % 2 == 0 else 96 for n in range(8)]
        for h in range(7):
            head = None
            for n in range(8):
                low = max(starts[n], 128 * h)
                high = min(starts[n] + sizes[n], 128 * h + 128)
                if low < high:
                    shift = (starts[n] - 128 * h) % 128
                    moved = pltpu.roll(pieces[n], shift, 1) if shift else pieces[n]
                    if head is None:
                        head = moved
                    else:
                        head = jnp.where(lane < low - 128 * h, head, moved)
            qf[at, pl.ds(h, 16, stride=8), :] = head

    local[0].wait()
    local[1].wait()
    for copy in local[3:]:
        copy.wait()
    for d in (2, 1, 3):
        arrived(kbuf.at[d], k_rs.at[d])
    for d in (2, 1, 3):
        arrived(vbuf.at[d], v_rs.at[d])

    sfx[gx] = sbuf[x, 2 * yh + c]
    for d in range(1, 16):
        to = (gx + d) % 16
        send(sbuf.at[to // 4, to % 4], sfx.at[gx], s_ss.at[d], s_rs.at[gx], (to, gy))

    for dy in (2, 1, 3, 0):
        to_y = (y + dy) % 4
        first = (to_y % 2) * 4 + (to_y // 2) * 2
        rows = qf[pl.ds(first, 2)].reshape(256, 128).astype(BF16)
        top = None
        for n in range(4):
            scores = lax.dot_general(rows, kbuf[n], ROW_DIMS, preferred_element_type=F32)
            s_ref[:, n * 512 : (n + 1) * 512] = scores
            for m in range(4):
                part = scores[:, m * 128 : (m + 1) * 128]
                top = part if top is None else jnp.maximum(top, part)
        top = (jnp.max(top, axis=1, keepdims=True) * SCALE).astype(BF16).astype(F32)
        total, values = 0.0, 0.0
        for n in range(4):
            probs = jnp.exp2(s_ref[:, n * 512 : (n + 1) * 512] * SCALE - top)
            for m in range(4):
                total = total + probs[:, m * 128 : (m + 1) * 128]
            values = values + jnp.dot(probs.astype(BF16), vbuf[n], preferred_element_type=F32)
        total = jnp.sum(total, axis=1, keepdims=True)
        packed = with_stats(
            values.reshape(32, 8, 128), top.reshape(32, 8, 1), total.reshape(32, 8, 1), True
        )
        osend[dy] = packed.reshape(2, 128, 128).astype(BF16)
        if dy:
            for to_c in range(2):
                send(
                    osend.at[dy, to_c], orecv.at[dy * 2 + c], o_ss.at[dy * 2 + to_c], o_rs.at[dy * 2 + c],
                    dev(y_=to_y, c_=to_c),
                )
        else:
            send(osend.at[0, 1 - c], orecv.at[c], o_ss.at[0], o_rs.at[c], dev(c_=1 - c))
            orecv[c] = osend[0, c]

    for d in range(1, 16):
        source = (gx + d) % 16
        arrived(sfx.at[source], s_rs.at[source])
    own = qf[mine, 64:72, :].astype(BF16)
    suffix_keys = sfx[:, 0].reshape(256, 128)
    suffix_values = sfx[:, 1].reshape(256, 128)
    scores = lax.dot_general(own, suffix_keys, ROW_DIMS, preferred_element_type=F32) * SCALE
    live = iota((8, 256), 1) < len_ref[2 * yh + c]
    scores = jnp.where(live, scores, -1e30)
    suffix_top = jnp.max(scores, axis=1, keepdims=True)
    probs = jnp.where(live, jnp.exp2(scores - suffix_top), 0.0)
    suffix_total = jnp.sum(probs, axis=1, keepdims=True)
    suffix_out = jnp.dot(probs.astype(BF16), suffix_values, preferred_element_type=F32)

    for dy in (2, 1, 3):
        for from_c in range(2):
            arrived(orecv.at[dy * 2 + from_c], o_rs.at[dy * 2 + from_c])
    arrived(orecv.at[1 - c], o_rs.at[1 - c])
    parts = []
    for n in range(8):
        tiles = orecv[n].astype(F32).reshape(16, 8, 128)
        parts.append((tiles,) + read_stats(tiles, True))
    zsend[...] = with_stats(*merge(parts), False)

    for p in (0, 1, 15, 2, 14, 3, 13, 4, 12, 5, 11, 6, 10, 7, 9):
        send(zsend.at[p], zrecv.at[p], z_ss.at[p], z_rs.at[p], dev(z_=(z + p + 8) % 16))
    zrecv[8] = zsend[8]
    for p in range(16):
        if p != 8:
            arrived(zrecv.at[p], z_rs.at[p])
    tiles = zrecv[...]
    tops, totals = read_stats(tiles, False)
    parts = [(tiles[p], tops[p], totals[p]) for p in range(16)]
    parts.append((suffix_out, suffix_top, suffix_total))
    values, _, total = merge(parts)
    heads = jnp.where(iota((8, 128), 0) < 7, values / total, 0.0)

    hbuf[2 * yh + c] = heads
    for at, (dyh, dc) in enumerate(((1, 0), (1, 1), (0, 1))):
        to = dev(y_=(y + 2 * dyh) % 4, c_=(c + dc) % 2)
        send(hbuf.at[2 * yh + c], hbuf.at[2 * yh + c], h_ss.at[at], h_rs.at[2 * yh + c], to)
    for dyh, dc in ((1, 0), (1, 1), (0, 1)):
        source = 2 * ((yh + dyh) % 2) + (c + dc) % 2
        arrived(hbuf.at[source], h_rs.at[source])

    feature = 224 * (2 * yh + c)
    head, off = feature // 128, feature % 128
    lane = iota((8, 128), 1)
    moved = []
    for n in range(3):
        four = jnp.concatenate([hbuf[t, pl.ds(head + n, 1), :] for t in range(4)], axis=0)
        eight = jnp.concatenate([four, four], axis=0)
        moved.append(pltpu.roll(eight, (128 - off) % 128, 1))
    left = jnp.where(lane < 128 - off, moved[0], moved[1])
    right = jnp.where(lane < 128 - off, moved[1], moved[2])
    right = jnp.where(lane < 96, right, 0.0)
    features = jnp.concatenate([left, right], axis=1).astype(BF16)
    row = iota((8, 128), 0)
    for d in tuple(range(1, 16)) + (0,):
        to = (gx + d) % 16
        product = jnp.dot(features, wp[to], preferred_element_type=F32)
        tile = jnp.where(row < 4, product[:, 0:128], product[:, 128:256])
        if d:
            psend[d] = tile
            send(psend.at[d], precv.at[d], p_ss.at[d], p_rs.at[d], (to, gy))
        else:
            result = tile
    for d in range(1, 16):
        arrived(precv.at[d], p_rs.at[d])
    for d in range(1, 16):
        result = result + precv[d]
    o_ref[:, 0:128] = result[0:4].astype(BF16)
    o_ref[:, 128:224] = result[4:8, 0:96].astype(BF16)
    for copy in sent:
        copy.wait_send()


def on_device(query, keys, values, suffix_keys, suffix_values, lengths, out_weight):
    hbm = pl.BlockSpec(memory_space=pltpu.HBM)
    dma = pltpu.SemaphoreType.DMA
    return pl.pallas_call(
        kernel,
        out_shape=jax.ShapeDtypeStruct((4, 224), BF16),
        in_specs=[hbm] * 7,
        out_specs=pl.BlockSpec(memory_space=pltpu.VMEM),
        scratch_shapes=[
            pltpu.VMEM((4, 224), BF16),
            pltpu.SMEM((4,), jnp.int32),
            pltpu.VMEM((4, 512, 128), BF16),
            pltpu.VMEM((4, 512, 128), BF16),
            pltpu.VMEM((224, 3584), BF16),
            pltpu.VMEM((16, 256, 256), BF16),
            pltpu.VMEM((4, 4, 2, 16, 128), BF16),
            pltpu.VMEM((16, 2, 16, 128), BF16),
            pltpu.VMEM((16, 8, 128), F32),
            pltpu.VMEM((128, 128), BF16),
            pltpu.VMEM((8, 128, 128), BF16),
            pltpu.VMEM((8, 128, 128), F32),
            pltpu.VMEM((8, 128, 128), F32),
            pltpu.VMEM((256, 2048), F32),
            pltpu.VMEM((4, 2, 128, 128), BF16),
            pltpu.VMEM((8, 128, 128), BF16),
            pltpu.VMEM((16, 8, 128), F32),
            pltpu.VMEM((16, 8, 128), F32),
            pltpu.VMEM((4, 8, 128), F32),
            pltpu.VMEM((16, 8, 128), F32),
            pltpu.VMEM((16, 8, 128), F32),
            dma((13,)),
            dma((4,)), dma((4,)), dma((4,)), dma((4,)),
            dma((16,)), dma((16,)),
            dma((16,)), dma((16,)),
            dma((3, 7)), dma((3, 8)),
            dma((8,)), dma((8,)),
            dma((16,)), dma((16,)),
            dma((3,)), dma((4,)),
            dma((16,)), dma((16,)),
        ],
        compiler_params=pltpu.CompilerParams(
            collective_id=0, has_side_effects=True, vmem_limit_bytes=56 * 2**20
        ),
        name="decode_attention",
    )(query, keys, values, suffix_keys, suffix_values, lengths, out_weight)


def solution(mesh):
    return jax.shard_map(
        on_device,
        mesh=mesh,
        in_specs=(
            P("gy", "gx"),
            P(("gx", "gy"), None),
            P(("gx", "gy"), None),
            P("gy", "gx", None),
            P("gy", "gx", None),
            P("gy"),
            P("gx", None),
        ),
        out_specs=P("gy", "gx"),
        check_vma=False,
    )
```

```python
import math

import jax
import jax.numpy as jnp
from jax import lax
from jax.experimental import pallas as pl
from jax.experimental.pallas import tpu as pltpu
from jax.sharding import PartitionSpec as P

MESH = pl.DeviceIdType.MESH
F32, BF16 = jnp.float32, jnp.bfloat16
HD = 128
SCALE = math.log2(math.e) / math.sqrt(HD)
ROW_DIMS = (((1,), (1,)), ((), ()))


def iota(shape, axis):
    return lax.broadcasted_iota(jnp.int32, shape, axis)


def spread(weights, selector):
    high = weights.astype(BF16).astype(F32)
    both = high + pltpu.roll(weights - high, 16, 1)
    wide = jnp.dot(both.astype(BF16), selector, preferred_element_type=F32)
    return wide[:, 0:128], wide[:, 128:256]


def stats(tops, totals, split):
    lane = iota((1, 128), 1)
    out = 0.0
    for i in range(3):
        out = out + jnp.where(lane == 96 + i, tops[i], 0.0)
        if split:
            high = totals[i].astype(BF16).astype(F32)
            out = out + jnp.where(lane == 100 + i, high, 0.0) + jnp.where(lane == 104 + i, totals[i] - high, 0.0)
        else:
            out = out + jnp.where(lane == 100 + i, totals[i], 0.0)
    return out


def kernel(
    q_hbm, k_hbm, v_hbm, sk_hbm, sv_hbm, len_hbm, w_hbm, o_ref,
    q_ref, len_ref, kbuf, vbuf, wraw, wp, sbuf, sfx, ztile, qsend, qall, xf, qf, s_ref,
    acc, tops, totals, selector, osend, orecv, zsend, zrecv, ssend, srecv, psend, precv,
    local_sem, k_ss, k_rs, v_ss, v_rs, s_ss, s_rs, r_ss, r_rs, f_ss,
    qa_ss, qa_rs, o_ss, o_rs, z_ss, z_rs, h_ss, h_rs, p_ss, p_rs,
):
    gx, gy = lax.axis_index("gx"), lax.axis_index("gy")
    x, yh, c = gx // 4, (gx // 2) % 2, gx % 2
    yl, z = gy // 16, gy % 16
    y = 2 * yh + yl

    def dev(x_=None, y_=None, c_=None, z_=None):
        x_ = x if x_ is None else x_
        y_ = y if y_ is None else y_
        c_ = c if c_ is None else c_
        z_ = z if z_ is None else z_
        return (x_ * 4 + (y_ // 2) * 2 + c_, (y_ % 2) * 16 + z_)

    def lanes(i):
        return pl.ds(pl.multiple_of(i * HD, HD), HD)

    sent = []

    def send(src, dst, ss, rs, to):
        copy = pltpu.make_async_remote_copy(
            src_ref=src, dst_ref=dst, send_sem=ss, recv_sem=rs, device_id=to, device_id_type=MESH
        )
        copy.start()
        sent.append(copy)

    def arrived(dst, rs):
        pltpu.make_async_remote_copy(
            src_ref=dst, dst_ref=dst, send_sem=rs, recv_sem=rs, device_id=dev(z_=(z + 1) % 16),
            device_id_type=MESH,
        ).wait_recv()

    around = [dev(z_=(z + hops) % 16) for hops in (1, 2, 3, 4, 12, 13, 14, 15)]
    around += [dev(x_=(x + d) % 4) for d in (1, 2, 3)]
    partners = [(dy, dc) for dy in (2, 1, 3, 0) for dc in (0, 1) if dy or dc]
    around += [dev(y_=(y + dy) % 4, c_=(c + dc) % 2) for dy, dc in partners]
    barrier = pltpu.get_barrier_semaphore()
    for to in around:
        pl.semaphore_signal(barrier, inc=1, device_id=to, device_id_type=MESH)

    local = [
        pltpu.make_async_copy(k_hbm.at[:, lanes(x)], kbuf.at[0], local_sem.at[0]),
        pltpu.make_async_copy(v_hbm.at[:, lanes(x)], vbuf.at[0], local_sem.at[1]),
        pltpu.make_async_copy(w_hbm, wraw, local_sem.at[2]),
    ]
    for g in range(4):
        for at, ref in enumerate((sk_hbm, sv_hbm)):
            local.append(
                pltpu.make_async_copy(
                    ref.at[:, :, g * HD : (g + 1) * HD], sbuf.at[g, :, at], local_sem.at[3 + 2 * g + at]
                )
            )
    local.append(pltpu.make_async_copy(len_hbm, len_ref, local_sem.at[11]))
    fetch = pltpu.make_async_copy(q_hbm, q_ref, local_sem.at[12])
    fetch.start()
    pl.semaphore_wait(barrier, len(around))

    for group in ((1, 3), (2,)):
        for d in group:
            to = (x + d) % 4
            send(k_hbm.at[:, lanes(to)], kbuf.at[d], k_ss.at[d], k_rs.at[d], dev(x_=to))
        for d in group:
            to = (x + d) % 4
            send(v_hbm.at[:, lanes(to)], vbuf.at[d], v_ss.at[d], v_rs.at[d], dev(x_=to))

    fetch.wait()
    query = q_ref[...].astype(F32)
    ztile[8] = jnp.zeros((8, 128), F32)
    ztile[8, pl.ds(0, 4, stride=2), :] = query[:, 0:128]
    ztile[8, pl.ds(1, 4, stride=2), 0:96] = query[:, 128:224]
    for hops in (4, 3, 2, 1):
        for way in (hops, -hops):
            to = dev(z_=(z + 16 + way) % 16)
            send(ztile.at[8], ztile.at[8 - way], r_ss.at[8 - way], r_rs.at[8 - way], to)
    for copy in local:
        copy.start()

    local[2].wait()
    wp[:, 224:256, :] = jnp.zeros((16, 32, 256), BF16)
    lane = iota((224, 128), 1)

    def relay(q, carry):
        for r in range(4):
            first, off = (224 * r) // 128, (224 * r) % 128
            tiles = []
            for n in range(3):
                if n < 2 or off >= 64:
                    at = pl.multiple_of(q * 896 + (first + n) * 128, 128)
                    tile = wraw[:, pl.ds(at, 128)].astype(F32)
                    tiles.append(pltpu.roll(tile, 128 - off, 1) if off else tile)
                else:
                    tiles.append(jnp.zeros((224, 128), F32))
            for n in range(2):
                block = jnp.where(lane < 128 - off, tiles[n], tiles[n + 1])
                wp[q * 4 + r, 0:224, n * 128 : (n + 1) * 128] = block.astype(BF16)
        return carry

    lax.fori_loop(0, 4, relay, 0)

    offset = (224 * (2 * yh + c)) % 128
    at, feature = iota((128, 256), 0), iota((128, 256), 1)
    head = 96 + ((feature + offset) >> 7)
    chosen = ((at == head) | (at == head + 16)) & (feature < 224)
    selector[...] = jnp.where(chosen, 1.0, 0.0).astype(BF16)

    mine = yl * 4 + 2 * yh + c

    def pass_on(p):
        @pl.when((p >= 4) & (p != 8) & (p <= 12))
        def _():
            arrived(ztile.at[p], r_rs.at[p])

        def forward(to_p, way):
            pltpu.make_async_remote_copy(
                src_ref=ztile.at[p], dst_ref=ztile.at[to_p], send_sem=f_ss, recv_sem=r_rs.at[to_p],
                device_id=dev(z_=(z + 16 + way) % 16), device_id_type=MESH,
            ).start()

        @pl.when((p >= 4) & (p <= 7))
        def _():
            forward(p - 4, 4)

        @pl.when((p >= 9) & (p <= 11))
        def _():
            forward(p + 4, -4)

    def slot_of(zs):
        return (zs - z + 24) % 16

    for zs in range(16):
        pass_on(slot_of(zs))
    for half in range(2):
        for zs in range(8 * half, 8 * half + 8):
            p = slot_of(zs)

            @pl.when((p < 4) | (p > 12))
            def _():
                arrived(ztile.at[p], r_rs.at[p])

        rows = pl.ds(64 * half, 64)
        for zs in range(8 * half, 8 * half + 8):
            xf[0, 8 * zs : 8 * zs + 8, :] = ztile[slot_of(zs)]
        packed = xf[0, rows, :].astype(BF16)
        qall[mine, rows, :] = packed
        qsend[rows, :] = packed
        for at, (dy, dc) in enumerate(partners):
            send(
                qsend.at[rows], qall.at[mine, rows], qa_ss.at[half, at], qa_rs.at[half, mine],
                dev(y_=(y + dy) % 4, c_=(c + dc) % 2),
            )

    def by_head(half):
        for dy, dc in partners:
            source = (y + dy) % 4
            source = (source % 2) * 4 + (source // 2) * 2 + (c + dc) % 2
            arrived(qall.at[source, pl.ds(64 * half, 64)], qa_rs.at[half, source])
        lane = iota((32, 128), 1)
        xf[:, 64 * half : 64 * half + 64, :] = qall[:, 64 * half : 64 * half + 64, :].astype(F32)
        for side in range(2):
            pieces = [xf[side * 4 + n // 2, pl.ds(64 * half + n % 2, 32, stride=2), :] for n in range(8)]
            starts = [224 * (n // 2) + 128 * (n % 2) for n in range(8)]
            sizes = [128 if n % 2 == 0 else 96 for n in range(8)]
            for h in range(7):
                head = None
                for n in range(8):
                    low = max(starts[n], 128 * h)
                    high = min(starts[n] + sizes[n], 128 * h + 128)
                    if low < high:
                        shift = (starts[n] - 128 * h) % 128
                        moved = pltpu.roll(pieces[n], shift, 1) if shift else pieces[n]
                        if head is None:
                            head = moved
                        else:
                            head = jnp.where(lane < low - 128 * h, head, moved)
                if h <= 3:
                    qf[half, side * 2, h * 32 : (h + 1) * 32, :] = head
                if h >= 3:
                    qf[half, side * 2 + 1, (h - 3) * 32 : (h - 2) * 32, :] = head

    def attend(half, chunks, old_top):
        rows = qf[half].reshape(512, 128).astype(BF16)
        top = None
        for n, k in enumerate(chunks):
            scores = lax.dot_general(rows, kbuf[k], ROW_DIMS, preferred_element_type=F32)
            s_ref[:, n * 512 : (n + 1) * 512] = scores
            for m in range(4):
                part = scores[:, m * 128 : (m + 1) * 128]
                top = part if top is None else jnp.maximum(top, part)
        top = (jnp.max(top, axis=1, keepdims=True) * SCALE).astype(BF16).astype(F32)
        top = jnp.broadcast_to(top, (512, 128))
        if old_top is not None:
            top = jnp.maximum(top, old_top)
        total, values = 0.0, 0.0
        for n, k in enumerate(chunks):
            probs = []
            for m in range(4):
                at = n * 512 + m * 128
                part = jnp.exp2(s_ref[:, at : at + 128] * SCALE - top)
                total = total + part
                probs.append(part.astype(BF16))
            probs = jnp.concatenate(probs, axis=1)
            values = values + jnp.dot(probs, vbuf[k], preferred_element_type=F32)
        return top, jnp.broadcast_to(jnp.sum(total, axis=1, keepdims=True), (512, 128)), values

    def keep(top, total, values):
        acc[...] = values.reshape(4, 128, 128)
        tops[...] = top.reshape(4, 128, 128)
        totals[...] = total.reshape(4, 128, 128)

    def to_owners(half):
        lane = iota((32, 128), 1)
        for n in range(4):
            to_y, to_yh = 2 * (n % 2) + n // 2, n % 2
            dy = (to_y - y + 4) % 4
            for to_c in range(2):
                start = 64 * to_yh + 224 * to_c
                off = start % 128
                js = [min(start // 128 + i, 3) for i in range(3)]
                picked = [[part[n, 32 * j : 32 * j + 32, :] for j in js] for part in (acc, tops, totals)]
                moved = [pltpu.roll(part, 128 - off, 1) if off else part for part in picked[0]]
                first = jnp.where(lane < 128 - off, moved[0], moved[1])
                osend[half, n, to_c, 0:32, :] = first.astype(BF16)
                second = jnp.where(lane < 128 - off, moved[1], moved[2])
                second = jnp.where(lane < 96, second, stats(picked[1], picked[2], True))
                osend[half, n, to_c, 32:64, :] = second.astype(BF16)
                here = (dy == 0) & (c == to_c)

                @pl.when(jnp.logical_not(here))
                def _():
                    pltpu.make_async_remote_copy(
                        src_ref=osend.at[half, n, to_c], dst_ref=orecv.at[half, dy * 2 + c], send_sem=o_ss.at[half],
                        recv_sem=o_rs.at[half, dy * 2 + c], device_id=dev(y_=to_y, c_=to_c), device_id_type=MESH,
                    ).start()

                @pl.when(here)
                def _():
                    orecv[half, c] = osend[half, n, to_c]

    lane = iota((1, 128), 1)
    is_top = (lane >= 96) & (lane < 99)
    own_tile = pl.ds(pl.multiple_of(8 * z, 8), 8)

    def merge_partners(half):
        for dy in (2, 1, 3):
            for from_c in range(2):
                arrived(orecv.at[half, dy * 2 + from_c], o_rs.at[half, dy * 2 + from_c])
        arrived(orecv.at[half, 1 - c], o_rs.at[half, 1 - c])
        firsts = [orecv[half, k, 0:32, :].astype(F32) for k in range(8)]
        seconds = [orecv[half, k, 32:64, :].astype(F32) for k in range(8)]
        top = seconds[0]
        for k in range(1, 8):
            top = jnp.maximum(top, seconds[k])
        weight = [jnp.where(is_top, jnp.exp2(part - top), 0.0) for part in seconds]
        wide = spread(jnp.concatenate(weight, axis=0), selector[...])
        first, second, total = 0.0, 0.0, 0.0
        for k in range(8):
            total = total + weight[k] * (pltpu.roll(seconds[k], 124, 1) + pltpu.roll(seconds[k], 120, 1))
            first = first + wide[0][32 * k : 32 * k + 32] * firsts[k]
            second = second + wide[1][32 * k : 32 * k + 32] * seconds[k]
        second = second + jnp.where(is_top, top, 0.0) + pltpu.roll(total, 4, 1)
        zsend[pl.ds(64 * half, 32, stride=2), :] = first
        zsend[pl.ds(64 * half + 1, 32, stride=2), :] = second
        for zs in range(8 * half, 8 * half + 8):

            @pl.when(z != zs)
            def _():
                pltpu.make_async_remote_copy(
                    src_ref=zsend.at[pl.ds(8 * zs, 8)], dst_ref=zrecv.at[own_tile], send_sem=z_ss, recv_sem=z_rs.at[z],
                    device_id=dev(z_=zs), device_id_type=MESH,
                ).start()

    by_head(0)
    local[0].wait()
    local[1].wait()
    for d in (1, 3):
        arrived(kbuf.at[d], k_rs.at[d])
        arrived(vbuf.at[d], v_rs.at[d])
    keep(*attend(0, (0, 1, 3), None))
    for copy in local[3:]:
        copy.wait()
    sfx[gx] = sbuf[x, 2 * yh + c]
    arrived(kbuf.at[2], k_rs.at[2])
    arrived(vbuf.at[2], v_rs.at[2])
    old_top = tops[...].reshape(512, 128)
    top, total, values = attend(0, (2,), old_top)
    scale = jnp.exp2(old_top - top)
    keep(
        top, total + scale * totals[...].reshape(512, 128), values + scale * acc[...].reshape(512, 128)
    )
    to_owners(0)

    for d in range(1, 16):
        to = (gx + d) % 16
        send(sbuf.at[to // 4, to % 4], sfx.at[gx], s_ss.at[d], s_rs.at[gx], (to, gy))

    by_head(1)
    keep(*attend(1, (0, 1, 2, 3), None))
    to_owners(1)

    merge_partners(0)

    for d in range(1, 16):
        source = (gx + d) % 16
        arrived(sfx.at[source], s_rs.at[source])
    mine = 2 * yh + c
    own = [qf[z // 8, yl * 2 + n, pl.ds((z % 8) * 4 + mine, 4, stride=32), :] for n in range(2)]
    own = jnp.concatenate(own, axis=0).astype(BF16)
    suffix_keys = sfx[:, 0].reshape(256, 128)
    suffix_values = sfx[:, 1].reshape(256, 128)
    scores = lax.dot_general(own, suffix_keys, ROW_DIMS, preferred_element_type=F32) * SCALE
    live = iota((8, 256), 1) < len_ref[mine]
    scores = jnp.where(live, scores, -1e30)
    top = jnp.max(scores, axis=1, keepdims=True)
    probs = jnp.where(live, jnp.exp2(scores - top), 0.0)
    total = jnp.sum(probs, axis=1, keepdims=True)
    values = jnp.dot(probs.astype(BF16), suffix_values, preferred_element_type=F32)
    for to in range(4):
        start = 64 * (to // 2) + 224 * (to % 2)
        off = start % 128
        picked = []
        for part in (values, top, total):
            rows = [4 * (to // 2) + min(start // 128 + i, 3) for i in range(3)]
            picked.append([part[row : row + 1] for row in rows])
        moved = [pltpu.roll(part, 128 - off, 1) if off else part for part in picked[0]]
        ssend[to, 0:1, :] = jnp.where(lane < 128 - off, moved[0], moved[1])
        second = jnp.where(lane < 128 - off, moved[1], moved[2])
        ssend[to, 1:2, :] = jnp.where(lane < 96, second, stats(picked[1], picked[2], False))
    near_by = ((1, 0), (1, 1), (0, 1))
    for at, (dyh, dc) in enumerate(near_by):
        to_yh, to_c = (yh + dyh) % 2, (c + dc) % 2
        to = dev(y_=(y + 2 * dyh) % 4, c_=to_c)
        send(ssend.at[2 * to_yh + to_c], srecv.at[mine], h_ss.at[at], h_rs.at[mine], to)
    srecv[mine] = ssend[mine]

    merge_partners(1)
    zrecv[own_tile, :] = zsend[own_tile, :]
    for dyh, dc in near_by:
        source = 2 * ((yh + dyh) % 2) + (c + dc) % 2
        arrived(srecv.at[source], h_rs.at[source])
    tail = iota((8, 128), 0) < 4
    zeros = jnp.zeros((4, 128), F32)
    suffix_first = jnp.concatenate([srecv[t, 0:1, :] for t in range(4)] + [zeros], axis=0)
    suffix_second = jnp.concatenate([srecv[t, 1:2, :] for t in range(4)] + [zeros], axis=0)
    suffix_second = jnp.where(tail | jnp.logical_not(is_top), suffix_second, -1e30)

    for copy in sent:
        copy.wait_send()
    sent.clear()
    pltpu.make_async_remote_copy(
        src_ref=ztile.at[pl.ds(0, 7)], dst_ref=ztile.at[pl.ds(0, 7)], send_sem=f_ss, recv_sem=r_rs.at[8],
        device_id=dev(c_=1 - c), device_id_type=MESH,
    ).wait_send()

    for half in range(2):
        pltpu.make_async_remote_copy(
            src_ref=orecv.at[half, pl.ds(0, 7)], dst_ref=orecv.at[half, pl.ds(0, 7)], send_sem=o_ss.at[half],
            recv_sem=o_rs.at[half, 0], device_id=dev(c_=1 - c), device_id_type=MESH,
        ).wait_send()

    for hops in range(1, 16):
        source = (z + hops) % 16
        arrived(zrecv.at[pl.ds(pl.multiple_of(8 * source, 8), 8)], z_rs.at[source])
    first = zrecv[pl.ds(0, 64, stride=2), :]
    second = zrecv[pl.ds(1, 64, stride=2), :]
    firsts = [first[8 * k : 8 * k + 8] for k in range(8)] + [suffix_first]
    seconds = [second[8 * k : 8 * k + 8] for k in range(8)] + [suffix_second]
    top = seconds[0]
    for k in range(1, 9):
        top = jnp.maximum(top, seconds[k])
    top = jnp.maximum(top, pltpu.roll(top, 4, 0))
    weight = [jnp.where(is_top, jnp.exp2(part - top), 0.0) for part in seconds]
    wide = spread(jnp.concatenate(weight, axis=0), selector[...])
    first, second, total = 0.0, 0.0, 0.0
    for k in range(9):
        first = first + wide[0][8 * k : 8 * k + 8] * firsts[k]
        second = second + wide[1][8 * k : 8 * k + 8] * seconds[k]
        total = total + weight[k] * pltpu.roll(seconds[k], 124, 1)
    first = first + pltpu.roll(first, 4, 0)
    second = second + pltpu.roll(second, 4, 0)
    total = total + pltpu.roll(total, 4, 0)
    wide = spread(total, selector[...])
    second = jnp.where(lane < 96, second / wide[1], 0.0)
    features = jnp.concatenate([first / wide[0], second], axis=1).astype(BF16)

    row = iota((8, 128), 0)
    others = [(dx, dyh, dc) for dx in range(4) for dyh in range(2) for dc in range(2)]
    others.sort(key=lambda move: -(min(move[0], 4 - move[0]) + 2 * move[1] + move[2]))
    for at, (dx, dyh, dc) in enumerate(others):
        to = ((x + dx) % 4) * 4 + ((yh + dyh) % 2) * 2 + (c + dc) % 2
        product = jnp.dot(features, wp[to], preferred_element_type=F32)
        tile = jnp.where(row < 4, product[:, 0:128], product[:, 128:256])
        if at < 15:
            psend[at] = tile
            send(psend.at[at], precv.at[at], p_ss.at[at], p_rs.at[at], (to, gy))
    for at in range(15):
        arrived(precv.at[at], p_rs.at[at])
    for at in range(15):
        tile = tile + precv[at]
    pltpu.make_async_remote_copy(
        src_ref=zsend.at[pl.ds(0, 120)], dst_ref=zsend.at[pl.ds(0, 120)], send_sem=z_ss, recv_sem=z_rs.at[0],
        device_id=dev(c_=1 - c), device_id_type=MESH,
    ).wait_send()
    result = tile
    o_ref[:, 0:128] = result[0:4].astype(BF16)
    o_ref[:, 128:224] = result[4:8, 0:96].astype(BF16)
    for copy in sent:
        copy.wait_send()


def on_device(query, keys, values, suffix_keys, suffix_values, lengths, out_weight):
    hbm = pl.BlockSpec(memory_space=pltpu.HBM)
    dma = pltpu.SemaphoreType.DMA
    return pl.pallas_call(
        kernel,
        out_shape=jax.ShapeDtypeStruct((4, 224), BF16),
        in_specs=[hbm] * 7,
        out_specs=pl.BlockSpec(memory_space=pltpu.VMEM),
        scratch_shapes=[
            pltpu.VMEM((4, 224), BF16),
            pltpu.SMEM((4,), jnp.int32),
            pltpu.VMEM((4, 512, 128), BF16),
            pltpu.VMEM((4, 512, 128), BF16),
            pltpu.VMEM((224, 3584), BF16),
            pltpu.VMEM((16, 256, 256), BF16),
            pltpu.VMEM((4, 4, 2, 16, 128), BF16),
            pltpu.VMEM((16, 2, 16, 128), BF16),
            pltpu.VMEM((16, 8, 128), F32),
            pltpu.VMEM((128, 128), BF16),
            pltpu.VMEM((8, 128, 128), BF16),
            pltpu.VMEM((8, 128, 128), F32),
            pltpu.VMEM((2, 4, 128, 128), F32),
            pltpu.VMEM((512, 2048), F32),
            pltpu.VMEM((4, 128, 128), F32),
            pltpu.VMEM((4, 128, 128), F32),
            pltpu.VMEM((4, 128, 128), F32),
            pltpu.VMEM((128, 256), BF16),
            pltpu.VMEM((2, 4, 2, 64, 128), BF16),
            pltpu.VMEM((2, 8, 64, 128), BF16),
            pltpu.VMEM((128, 128), F32),
            pltpu.VMEM((128, 128), F32),
            pltpu.VMEM((4, 8, 128), F32),
            pltpu.VMEM((4, 8, 128), F32),
            pltpu.VMEM((16, 8, 128), F32),
            pltpu.VMEM((16, 8, 128), F32),
            dma((13,)),
            dma((4,)), dma((4,)), dma((4,)), dma((4,)),
            dma((16,)), dma((16,)),
            dma((16,)), dma((16,)), dma,
            dma((2, 7)), dma((2, 8)),
            dma((2,)), dma((2, 8)),
            dma, dma((16,)),
            dma((3,)), dma((4,)),
            dma((16,)), dma((16,)),
        ],
        compiler_params=pltpu.CompilerParams(
            collective_id=0, has_side_effects=True, vmem_limit_bytes=56 * 2**20
        ),
        name="decode_attention",
    )(query, keys, values, suffix_keys, suffix_values, lengths, out_weight)


def solution(mesh):
    return jax.shard_map(
        on_device,
        mesh=mesh,
        in_specs=(
            P("gy", "gx"),
            P(("gx", "gy"), None),
            P(("gx", "gy"), None),
            P("gy", "gx", None),
            P("gy", "gx", None),
            P("gy"),
            P("gx", None),
        ),
        out_specs=P("gy", "gx"),
        check_vma=False,
    )
```

```python
import math

import jax
import jax.numpy as jnp
from jax import lax
from jax.experimental import pallas as pl
from jax.experimental.pallas import tpu as pltpu
from jax.sharding import PartitionSpec as P

MESH = pl.DeviceIdType.MESH
F32, BF16 = jnp.float32, jnp.bfloat16
HD = 128
SCALE = math.log2(math.e) / math.sqrt(HD)
ROW_DIMS = (((1,), (1,)), ((), ()))


def iota(shape, axis):
    return lax.broadcasted_iota(jnp.int32, shape, axis)


def spread(weights, selector):
    high = weights.astype(BF16).astype(F32)
    both = high + pltpu.roll(weights - high, 16, 1)
    wide = jnp.dot(both.astype(BF16), selector, preferred_element_type=F32)
    return wide[:, 0:128], wide[:, 128:256]


def stats(tops, totals, split):
    lane = iota((1, 128), 1)
    out = 0.0
    for i in range(3):
        out = out + jnp.where(lane == 96 + i, tops[i], 0.0)
        if split:
            high = totals[i].astype(BF16).astype(F32)
            out = out + jnp.where(lane == 100 + i, high, 0.0) + jnp.where(lane == 104 + i, totals[i] - high, 0.0)
        else:
            out = out + jnp.where(lane == 100 + i, totals[i], 0.0)
    return out


def kernel(
    q_hbm, k_hbm, v_hbm, sk_hbm, sv_hbm, len_hbm, w_hbm, o_ref,
    q_ref, len_ref, kbuf, vbuf, wraw, wp, sbuf, sfx, ztile, qsend, qall, xf, qf, s_ref,
    acc, tops, totals, selector, osend, orecv, zsend, zrecv, ssend, srecv, psend, precv,
    local_sem, k_ss, k_rs, v_ss, v_rs, s_ss, s_rs, r_ss, r_rs, f_ss,
    qa_ss, qa_rs, o_ss, o_rs, z_ss, z_rs, h_ss, h_rs, p_ss, p_rs,
):
    gx, gy = lax.axis_index("gx"), lax.axis_index("gy")
    x, yh, c = gx // 4, (gx // 2) % 2, gx % 2
    yl, z = gy // 16, gy % 16
    y = 2 * yh + yl

    def dev(x_=None, y_=None, c_=None, z_=None):
        x_ = x if x_ is None else x_
        y_ = y if y_ is None else y_
        c_ = c if c_ is None else c_
        z_ = z if z_ is None else z_
        return (x_ * 4 + (y_ // 2) * 2 + c_, (y_ % 2) * 16 + z_)

    def lanes(i):
        return pl.ds(pl.multiple_of(i * HD, HD), HD)

    sent = []

    def send(src, dst, ss, rs, to):
        copy = pltpu.make_async_remote_copy(
            src_ref=src, dst_ref=dst, send_sem=ss, recv_sem=rs, device_id=to, device_id_type=MESH
        )
        copy.start()
        sent.append(copy)

    def arrived(dst, rs):
        pltpu.make_async_remote_copy(
            src_ref=dst, dst_ref=dst, send_sem=rs, recv_sem=rs, device_id=dev(z_=(z + 1) % 16),
            device_id_type=MESH,
        ).wait_recv()

    around = [dev(z_=(z + hops) % 16) for hops in (1, 2, 3, 4, 12, 13, 14, 15)]
    around += [dev(x_=(x + d) % 4) for d in (1, 2, 3)]
    partners = [(dy, dc) for dy in (2, 1, 3, 0) for dc in (0, 1) if dy or dc]
    around += [dev(y_=(y + dy) % 4, c_=(c + dc) % 2) for dy, dc in partners]
    barrier = pltpu.get_barrier_semaphore()
    for to in around:
        pl.semaphore_signal(barrier, inc=1, device_id=to, device_id_type=MESH)

    local = [
        pltpu.make_async_copy(k_hbm.at[:, lanes(x)], kbuf.at[0], local_sem.at[0]),
        pltpu.make_async_copy(v_hbm.at[:, lanes(x)], vbuf.at[0], local_sem.at[1]),
        pltpu.make_async_copy(w_hbm, wraw, local_sem.at[2]),
    ]
    for g in range(4):
        for at, ref in enumerate((sk_hbm, sv_hbm)):
            local.append(
                pltpu.make_async_copy(
                    ref.at[:, :, g * HD : (g + 1) * HD], sbuf.at[g, :, at], local_sem.at[3 + 2 * g + at]
                )
            )
    local.append(pltpu.make_async_copy(len_hbm, len_ref, local_sem.at[11]))
    fetch = pltpu.make_async_copy(q_hbm, q_ref, local_sem.at[12])
    fetch.start()
    pl.semaphore_wait(barrier, len(around))

    for group in ((1, 3), (2,)):
        for d in group:
            to = (x + d) % 4
            send(k_hbm.at[:, lanes(to)], kbuf.at[d], k_ss.at[d], k_rs.at[d], dev(x_=to))
        for d in group:
            to = (x + d) % 4
            send(v_hbm.at[:, lanes(to)], vbuf.at[d], v_ss.at[d], v_rs.at[d], dev(x_=to))

    fetch.wait()
    query = q_ref[...].astype(F32)
    ztile[8] = jnp.zeros((8, 128), F32)
    ztile[8, pl.ds(0, 4, stride=2), :] = query[:, 0:128]
    ztile[8, pl.ds(1, 4, stride=2), 0:96] = query[:, 128:224]
    for hops in (4, 3, 2, 1):
        for way in (hops, -hops):
            to = dev(z_=(z + 16 + way) % 16)
            send(ztile.at[8], ztile.at[8 - way], r_ss.at[8 - way], r_rs.at[8 - way], to)
    for copy in local:
        copy.start()

    local[2].wait()
    wp[:, 224:256, :] = jnp.zeros((16, 32, 256), BF16)
    lane = iota((224, 128), 1)

    def relay(q, carry):
        for r in range(4):
            first, off = (224 * r) // 128, (224 * r) % 128
            tiles = []
            for n in range(3):
                if n < 2 or off >= 64:
                    at = pl.multiple_of(q * 896 + (first + n) * 128, 128)
                    tile = wraw[:, pl.ds(at, 128)].astype(F32)
                    tiles.append(pltpu.roll(tile, 128 - off, 1) if off else tile)
                else:
                    tiles.append(jnp.zeros((224, 128), F32))
            for n in range(2):
                block = jnp.where(lane < 128 - off, tiles[n], tiles[n + 1])
                wp[q * 4 + r, 0:224, n * 128 : (n + 1) * 128] = block.astype(BF16)
        return carry

    lax.fori_loop(0, 4, relay, 0)

    offset = (224 * (2 * yh + c)) % 128
    at, feature = iota((128, 256), 0), iota((128, 256), 1)
    head = 96 + ((feature + offset) >> 7)
    chosen = ((at == head) | (at == head + 16)) & (feature < 224)
    selector[...] = jnp.where(chosen, 1.0, 0.0).astype(BF16)

    mine = yl * 4 + 2 * yh + c

    def pass_on(p):
        @pl.when((p >= 4) & (p != 8) & (p <= 12))
        def _():
            arrived(ztile.at[p], r_rs.at[p])

        def forward(to_p, way):
            pltpu.make_async_remote_copy(
                src_ref=ztile.at[p], dst_ref=ztile.at[to_p], send_sem=f_ss, recv_sem=r_rs.at[to_p],
                device_id=dev(z_=(z + 16 + way) % 16), device_id_type=MESH,
            ).start()

        @pl.when((p >= 4) & (p <= 7))
        def _():
            forward(p - 4, 4)

        @pl.when((p >= 9) & (p <= 11))
        def _():
            forward(p + 4, -4)

    def slot_of(zs):
        return (zs - z + 24) % 16

    for zs in range(16):
        pass_on(slot_of(zs))
    for half in range(2):
        for zs in range(8 * half, 8 * half + 8):
            p = slot_of(zs)

            @pl.when((p < 4) | (p > 12))
            def _():
                arrived(ztile.at[p], r_rs.at[p])

        rows = pl.ds(64 * half, 64)
        for zs in range(8 * half, 8 * half + 8):
            xf[0, 8 * zs : 8 * zs + 8, :] = ztile[slot_of(zs)]
        packed = xf[0, rows, :].astype(BF16)
        qall[mine, rows, :] = packed
        qsend[rows, :] = packed
        for at, (dy, dc) in enumerate(partners):
            send(
                qsend.at[rows], qall.at[mine, rows], qa_ss.at[half, at], qa_rs.at[half, mine],
                dev(y_=(y + dy) % 4, c_=(c + dc) % 2),
            )

    def by_head(half):
        for dy, dc in partners:
            source = (y + dy) % 4
            source = (source % 2) * 4 + (source // 2) * 2 + (c + dc) % 2
            arrived(qall.at[source, pl.ds(64 * half, 64)], qa_rs.at[half, source])
        lane = iota((32, 128), 1)
        xf[:, 64 * half : 64 * half + 64, :] = qall[:, 64 * half : 64 * half + 64, :].astype(F32)
        for side in range(2):
            pieces = [xf[side * 4 + n // 2, pl.ds(64 * half + n % 2, 32, stride=2), :] for n in range(8)]
            starts = [224 * (n // 2) + 128 * (n % 2) for n in range(8)]
            sizes = [128 if n % 2 == 0 else 96 for n in range(8)]
            for h in range(7):
                head = None
                for n in range(8):
                    low = max(starts[n], 128 * h)
                    high = min(starts[n] + sizes[n], 128 * h + 128)
                    if low < high:
                        shift = (starts[n] - 128 * h) % 128
                        moved = pltpu.roll(pieces[n], shift, 1) if shift else pieces[n]
                        if head is None:
                            head = moved
                        else:
                            head = jnp.where(lane < low - 128 * h, head, moved)
                if h <= 3:
                    qf[half, side * 2, h * 32 : (h + 1) * 32, :] = head
                if h >= 3:
                    qf[half, side * 2 + 1, (h - 3) * 32 : (h - 2) * 32, :] = head

    def attend(half, chunks, old_top):
        rows = qf[half].reshape(512, 128).astype(BF16)
        top = None
        for n, k in enumerate(chunks):
            scores = lax.dot_general(rows, kbuf[k], ROW_DIMS, preferred_element_type=F32)
            s_ref[:, n * 512 : (n + 1) * 512] = scores
            for m in range(4):
                part = scores[:, m * 128 : (m + 1) * 128]
                top = part if top is None else jnp.maximum(top, part)
        top = (jnp.max(top, axis=1, keepdims=True) * SCALE).astype(BF16).astype(F32)
        top = jnp.broadcast_to(top, (512, 128))
        if old_top is not None:
            top = jnp.maximum(top, old_top)
        total, values = 0.0, 0.0
        for n, k in enumerate(chunks):
            probs = []
            for m in range(4):
                at = n * 512 + m * 128
                part = jnp.exp2(s_ref[:, at : at + 128] * SCALE - top)
                total = total + part
                probs.append(part.astype(BF16))
            probs = jnp.concatenate(probs, axis=1)
            values = values + jnp.dot(probs, vbuf[k], preferred_element_type=F32)
        return top, jnp.broadcast_to(jnp.sum(total, axis=1, keepdims=True), (512, 128)), values

    def keep(top, total, values):
        acc[...] = values.reshape(4, 128, 128)
        tops[...] = top.reshape(4, 128, 128)
        totals[...] = total.reshape(4, 128, 128)

    def to_owners(half):
        lane = iota((32, 128), 1)
        for n in range(4):
            to_y, to_yh = 2 * (n % 2) + n // 2, n % 2
            dy = (to_y - y + 4) % 4
            for to_c in range(2):
                start = 64 * to_yh + 224 * to_c
                off = start % 128
                js = [min(start // 128 + i, 3) for i in range(3)]
                picked = [[part[n, 32 * j : 32 * j + 32, :] for j in js] for part in (acc, tops, totals)]
                moved = [pltpu.roll(part, 128 - off, 1) if off else part for part in picked[0]]
                first = jnp.where(lane < 128 - off, moved[0], moved[1])
                osend[half, n, to_c, 0:32, :] = first.astype(BF16)
                second = jnp.where(lane < 128 - off, moved[1], moved[2])
                second = jnp.where(lane < 96, second, stats(picked[1], picked[2], True))
                osend[half, n, to_c, 32:64, :] = second.astype(BF16)
                here = (dy == 0) & (c == to_c)

                @pl.when(jnp.logical_not(here))
                def _():
                    pltpu.make_async_remote_copy(
                        src_ref=osend.at[half, n, to_c], dst_ref=orecv.at[half, dy * 2 + c], send_sem=o_ss.at[half],
                        recv_sem=o_rs.at[half, dy * 2 + c], device_id=dev(y_=to_y, c_=to_c), device_id_type=MESH,
                    ).start()

                @pl.when(here)
                def _():
                    orecv[half, c] = osend[half, n, to_c]

    lane = iota((1, 128), 1)
    is_top = (lane >= 96) & (lane < 99)
    own_tile = pl.ds(pl.multiple_of(8 * z, 8), 8)

    def merge_partners(half):
        for dy in (2, 1, 3):
            for from_c in range(2):
                arrived(orecv.at[half, dy * 2 + from_c], o_rs.at[half, dy * 2 + from_c])
        arrived(orecv.at[half, 1 - c], o_rs.at[half, 1 - c])
        firsts = [orecv[half, k, 0:32, :].astype(F32) for k in range(8)]
        seconds = [orecv[half, k, 32:64, :].astype(F32) for k in range(8)]
        top = seconds[0]
        for k in range(1, 8):
            top = jnp.maximum(top, seconds[k])
        weight = [jnp.where(is_top, jnp.exp2(part - top), 0.0) for part in seconds]
        wide = spread(jnp.concatenate(weight, axis=0), selector[...])
        first, second, total = 0.0, 0.0, 0.0
        for k in range(8):
            total = total + weight[k] * (pltpu.roll(seconds[k], 124, 1) + pltpu.roll(seconds[k], 120, 1))
            first = first + wide[0][32 * k : 32 * k + 32] * firsts[k]
            second = second + wide[1][32 * k : 32 * k + 32] * seconds[k]
        second = second + jnp.where(is_top, top, 0.0) + pltpu.roll(total, 4, 1)
        zsend[pl.ds(64 * half, 32, stride=2), :] = first
        zsend[pl.ds(64 * half + 1, 32, stride=2), :] = second
        for zs in range(8 * half, 8 * half + 8):

            @pl.when(z != zs)
            def _():
                pltpu.make_async_remote_copy(
                    src_ref=zsend.at[pl.ds(8 * zs, 8)], dst_ref=zrecv.at[own_tile], send_sem=z_ss, recv_sem=z_rs.at[z],
                    device_id=dev(z_=zs), device_id_type=MESH,
                ).start()

    local[0].wait()
    local[1].wait()
    for copy in local[3:]:
        copy.wait()
    for d in (1, 3):
        arrived(kbuf.at[d], k_rs.at[d])
        arrived(vbuf.at[d], v_rs.at[d])

    def send_suffix(dx, to_yh, to_c):
        to_x, slot = (x + dx) % 4, dx * 4 + (yh + to_yh) % 2 * 2 + (c + to_c) % 2
        to_yh, to_c = (yh + to_yh) % 2, (c + to_c) % 2
        send(
            sbuf.at[to_x, 2 * to_yh + to_c], sfx.at[gx], s_ss.at[slot], s_rs.at[gx],
            (to_x * 4 + 2 * to_yh + to_c, gy),
        )

    sfx[gx] = sbuf[x, 2 * yh + c]
    for dx in (1, 3, 0):
        for to_yh in range(2):
            for to_c in range(2):
                if dx or to_yh or to_c:
                    send_suffix(dx, to_yh, to_c)

    by_head(0)
    keep(*attend(0, (0, 1, 3), None))
    arrived(kbuf.at[2], k_rs.at[2])
    arrived(vbuf.at[2], v_rs.at[2])
    old_top = tops[...].reshape(512, 128)
    top, total, values = attend(0, (2,), old_top)
    scale = jnp.exp2(old_top - top)
    keep(
        top, total + scale * totals[...].reshape(512, 128), values + scale * acc[...].reshape(512, 128)
    )
    to_owners(0)

    for to_yh in range(2):
        for to_c in range(2):
            send_suffix(2, to_yh, to_c)

    by_head(1)
    keep(*attend(1, (0, 1, 2, 3), None))
    to_owners(1)

    merge_partners(0)

    for d in range(1, 16):
        source = (gx + d) % 16
        arrived(sfx.at[source], s_rs.at[source])
    mine = 2 * yh + c
    own = [qf[z // 8, yl * 2 + n, pl.ds((z % 8) * 4 + mine, 4, stride=32), :] for n in range(2)]
    own = jnp.concatenate(own, axis=0).astype(BF16)
    suffix_keys = sfx[:, 0].reshape(256, 128)
    suffix_values = sfx[:, 1].reshape(256, 128)
    scores = lax.dot_general(own, suffix_keys, ROW_DIMS, preferred_element_type=F32) * SCALE
    live = iota((8, 256), 1) < len_ref[mine]
    scores = jnp.where(live, scores, -1e30)
    top = jnp.max(scores, axis=1, keepdims=True)
    probs = jnp.where(live, jnp.exp2(scores - top), 0.0)
    total = jnp.sum(probs, axis=1, keepdims=True)
    values = jnp.dot(probs.astype(BF16), suffix_values, preferred_element_type=F32)
    for to in range(4):
        start = 64 * (to // 2) + 224 * (to % 2)
        off = start % 128
        picked = []
        for part in (values, top, total):
            rows = [4 * (to // 2) + min(start // 128 + i, 3) for i in range(3)]
            picked.append([part[row : row + 1] for row in rows])
        moved = [pltpu.roll(part, 128 - off, 1) if off else part for part in picked[0]]
        ssend[to, 0:1, :] = jnp.where(lane < 128 - off, moved[0], moved[1])
        second = jnp.where(lane < 128 - off, moved[1], moved[2])
        ssend[to, 1:2, :] = jnp.where(lane < 96, second, stats(picked[1], picked[2], False))
    near_by = ((1, 0), (1, 1), (0, 1))
    for at, (dyh, dc) in enumerate(near_by):
        to_yh, to_c = (yh + dyh) % 2, (c + dc) % 2
        to = dev(y_=(y + 2 * dyh) % 4, c_=to_c)
        send(ssend.at[2 * to_yh + to_c], srecv.at[mine], h_ss.at[at], h_rs.at[mine], to)
    srecv[mine] = ssend[mine]

    merge_partners(1)
    zrecv[own_tile, :] = zsend[own_tile, :]
    for dyh, dc in near_by:
        source = 2 * ((yh + dyh) % 2) + (c + dc) % 2
        arrived(srecv.at[source], h_rs.at[source])
    tail = iota((8, 128), 0) < 4
    zeros = jnp.zeros((4, 128), F32)
    suffix_first = jnp.concatenate([srecv[t, 0:1, :] for t in range(4)] + [zeros], axis=0)
    suffix_second = jnp.concatenate([srecv[t, 1:2, :] for t in range(4)] + [zeros], axis=0)
    suffix_second = jnp.where(tail | jnp.logical_not(is_top), suffix_second, -1e30)

    for copy in sent:
        copy.wait_send()
    sent.clear()
    pltpu.make_async_remote_copy(
        src_ref=ztile.at[pl.ds(0, 7)], dst_ref=ztile.at[pl.ds(0, 7)], send_sem=f_ss, recv_sem=r_rs.at[8],
        device_id=dev(c_=1 - c), device_id_type=MESH,
    ).wait_send()

    for half in range(2):
        pltpu.make_async_remote_copy(
            src_ref=orecv.at[half, pl.ds(0, 7)], dst_ref=orecv.at[half, pl.ds(0, 7)], send_sem=o_ss.at[half],
            recv_sem=o_rs.at[half, 0], device_id=dev(c_=1 - c), device_id_type=MESH,
        ).wait_send()

    for hops in range(1, 16):
        source = (z + hops) % 16
        arrived(zrecv.at[pl.ds(pl.multiple_of(8 * source, 8), 8)], z_rs.at[source])
    first = zrecv[pl.ds(0, 64, stride=2), :]
    second = zrecv[pl.ds(1, 64, stride=2), :]
    firsts = [first[8 * k : 8 * k + 8] for k in range(8)] + [suffix_first]
    seconds = [second[8 * k : 8 * k + 8] for k in range(8)] + [suffix_second]
    top = seconds[0]
    for k in range(1, 9):
        top = jnp.maximum(top, seconds[k])
    top = jnp.maximum(top, pltpu.roll(top, 4, 0))
    weight = [jnp.where(is_top, jnp.exp2(part - top), 0.0) for part in seconds]
    wide = spread(jnp.concatenate(weight, axis=0), selector[...])
    first, second, total = 0.0, 0.0, 0.0
    for k in range(9):
        first = first + wide[0][8 * k : 8 * k + 8] * firsts[k]
        second = second + wide[1][8 * k : 8 * k + 8] * seconds[k]
        total = total + weight[k] * pltpu.roll(seconds[k], 124, 1)
    first = first + pltpu.roll(first, 4, 0)
    second = second + pltpu.roll(second, 4, 0)
    total = total + pltpu.roll(total, 4, 0)
    wide = spread(total, selector[...])
    second = jnp.where(lane < 96, second / wide[1], 0.0)
    features = jnp.concatenate([first / wide[0], second], axis=1).astype(BF16)

    row = iota((8, 128), 0)
    others = [(dx, dyh, dc) for dx in range(4) for dyh in range(2) for dc in range(2)]
    others.sort(key=lambda move: -(min(move[0], 4 - move[0]) + 2 * move[1] + move[2]))
    for at, (dx, dyh, dc) in enumerate(others):
        to = ((x + dx) % 4) * 4 + ((yh + dyh) % 2) * 2 + (c + dc) % 2
        product = jnp.dot(features, wp[to], preferred_element_type=F32)
        tile = jnp.where(row < 4, product[:, 0:128], product[:, 128:256])
        if at < 15:
            psend[at] = tile
            send(psend.at[at], precv.at[at], p_ss.at[at], p_rs.at[at], (to, gy))
    for at in range(15):
        arrived(precv.at[at], p_rs.at[at])
    for at in range(15):
        tile = tile + precv[at]
    pltpu.make_async_remote_copy(
        src_ref=zsend.at[pl.ds(0, 120)], dst_ref=zsend.at[pl.ds(0, 120)], send_sem=z_ss, recv_sem=z_rs.at[0],
        device_id=dev(c_=1 - c), device_id_type=MESH,
    ).wait_send()
    result = tile
    o_ref[:, 0:128] = result[0:4].astype(BF16)
    o_ref[:, 128:224] = result[4:8, 0:96].astype(BF16)
    for copy in sent:
        copy.wait_send()


def on_device(query, keys, values, suffix_keys, suffix_values, lengths, out_weight):
    hbm = pl.BlockSpec(memory_space=pltpu.HBM)
    dma = pltpu.SemaphoreType.DMA
    return pl.pallas_call(
        kernel,
        out_shape=jax.ShapeDtypeStruct((4, 224), BF16),
        in_specs=[hbm] * 7,
        out_specs=pl.BlockSpec(memory_space=pltpu.VMEM),
        scratch_shapes=[
            pltpu.VMEM((4, 224), BF16),
            pltpu.SMEM((4,), jnp.int32),
            pltpu.VMEM((4, 512, 128), BF16),
            pltpu.VMEM((4, 512, 128), BF16),
            pltpu.VMEM((224, 3584), BF16),
            pltpu.VMEM((16, 256, 256), BF16),
            pltpu.VMEM((4, 4, 2, 16, 128), BF16),
            pltpu.VMEM((16, 2, 16, 128), BF16),
            pltpu.VMEM((16, 8, 128), F32),
            pltpu.VMEM((128, 128), BF16),
            pltpu.VMEM((8, 128, 128), BF16),
            pltpu.VMEM((8, 128, 128), F32),
            pltpu.VMEM((2, 4, 128, 128), F32),
            pltpu.VMEM((512, 2048), F32),
            pltpu.VMEM((4, 128, 128), F32),
            pltpu.VMEM((4, 128, 128), F32),
            pltpu.VMEM((4, 128, 128), F32),
            pltpu.VMEM((128, 256), BF16),
            pltpu.VMEM((2, 4, 2, 64, 128), BF16),
            pltpu.VMEM((2, 8, 64, 128), BF16),
            pltpu.VMEM((128, 128), F32),
            pltpu.VMEM((128, 128), F32),
            pltpu.VMEM((4, 8, 128), F32),
            pltpu.VMEM((4, 8, 128), F32),
            pltpu.VMEM((16, 8, 128), F32),
            pltpu.VMEM((16, 8, 128), F32),
            dma((13,)),
            dma((4,)), dma((4,)), dma((4,)), dma((4,)),
            dma((16,)), dma((16,)),
            dma((16,)), dma((16,)), dma,
            dma((2, 7)), dma((2, 8)),
            dma((2,)), dma((2, 8)),
            dma, dma((16,)),
            dma((3,)), dma((4,)),
            dma((16,)), dma((16,)),
        ],
        compiler_params=pltpu.CompilerParams(
            collective_id=0, has_side_effects=True, vmem_limit_bytes=56 * 2**20
        ),
        name="decode_attention",
    )(query, keys, values, suffix_keys, suffix_values, lengths, out_weight)


def solution(mesh):
    return jax.shard_map(
        on_device,
        mesh=mesh,
        in_specs=(
            P("gy", "gx"),
            P(("gx", "gy"), None),
            P(("gx", "gy"), None),
            P("gy", "gx", None),
            P("gy", "gx", None),
            P("gy"),
            P("gx", None),
        ),
        out_specs=P("gy", "gx"),
        check_vma=False,
    )
```

```python
import math

import jax
import jax.numpy as jnp
from jax import lax
from jax.experimental import pallas as pl
from jax.experimental.pallas import tpu as pltpu
from jax.sharding import PartitionSpec as P

MESH = pl.DeviceIdType.MESH
F32, BF16 = jnp.float32, jnp.bfloat16
HD = 128
SCALE = math.log2(math.e) / math.sqrt(HD)
ROW_DIMS = (((1,), (1,)), ((), ()))


def iota(shape, axis):
    return lax.broadcasted_iota(jnp.int32, shape, axis)


def spread(weights, selector):
    high = weights.astype(BF16).astype(F32)
    both = high + pltpu.roll(weights - high, 16, 1)
    wide = jnp.dot(both.astype(BF16), selector, preferred_element_type=F32)
    return wide[:, 0:128], wide[:, 128:256]


def stats(tops, totals, split):
    lane = iota((1, 128), 1)
    out = 0.0
    for i in range(3):
        out = out + jnp.where(lane == 96 + i, tops[i], 0.0)
        if split:
            high = totals[i].astype(BF16).astype(F32)
            out = out + jnp.where(lane == 100 + i, high, 0.0) + jnp.where(lane == 104 + i, totals[i] - high, 0.0)
        else:
            out = out + jnp.where(lane == 100 + i, totals[i], 0.0)
    return out


def kernel(
    q_hbm, k_hbm, v_hbm, sk_hbm, sv_hbm, len_hbm, w_hbm, o_ref,
    q_ref, len_ref, kbuf, vbuf, wraw, wp, sbuf, sfx, ztile, qsend, qall, xf, qf, s_ref,
    acc, tops, totals, selector, osend, orecv, zsend, zrecv, ssend, srecv, psend, precv,
    local_sem, k_ss, k_rs, v_ss, v_rs, s_ss, s_rs, r_ss, r_rs, f_ss,
    qa_ss, qa_rs, o_ss, o_rs, z_ss, z_rs, h_ss, h_rs, p_ss, p_rs,
):
    gx, gy = lax.axis_index("gx"), lax.axis_index("gy")
    x, yh, c = gx // 4, (gx // 2) % 2, gx % 2
    yl, z = gy // 16, gy % 16
    y = 2 * yh + yl

    def dev(x_=None, y_=None, c_=None, z_=None):
        x_ = x if x_ is None else x_
        y_ = y if y_ is None else y_
        c_ = c if c_ is None else c_
        z_ = z if z_ is None else z_
        return (x_ * 4 + (y_ // 2) * 2 + c_, (y_ % 2) * 16 + z_)

    def lanes(i):
        return pl.ds(pl.multiple_of(i * HD, HD), HD)

    sent = []

    def send(src, dst, ss, rs, to):
        copy = pltpu.make_async_remote_copy(
            src_ref=src, dst_ref=dst, send_sem=ss, recv_sem=rs, device_id=to, device_id_type=MESH
        )
        copy.start()
        sent.append(copy)

    def arrived(dst, rs):
        pltpu.make_async_remote_copy(
            src_ref=dst, dst_ref=dst, send_sem=rs, recv_sem=rs, device_id=dev(z_=(z + 1) % 16),
            device_id_type=MESH,
        ).wait_recv()

    around = [dev(z_=(z + hops) % 16) for hops in (1, 2, 3, 4, 12, 13, 14, 15)]
    around += [dev(x_=(x + d) % 4) for d in (1, 2, 3)]
    partners = [(dy, dc) for dy in (2, 1, 3, 0) for dc in (0, 1) if dy or dc]
    around += [dev(y_=(y + dy) % 4, c_=(c + dc) % 2) for dy, dc in partners]
    barrier = pltpu.get_barrier_semaphore()
    for to in around:
        pl.semaphore_signal(barrier, inc=1, device_id=to, device_id_type=MESH)

    local = [
        pltpu.make_async_copy(k_hbm.at[:, lanes(x)], kbuf.at[0], local_sem.at[0]),
        pltpu.make_async_copy(v_hbm.at[:, lanes(x)], vbuf.at[0], local_sem.at[1]),
        pltpu.make_async_copy(w_hbm, wraw, local_sem.at[2]),
    ]
    for g in range(4):
        for at, ref in enumerate((sk_hbm, sv_hbm)):
            local.append(
                pltpu.make_async_copy(
                    ref.at[:, :, g * HD : (g + 1) * HD], sbuf.at[g, :, at], local_sem.at[3 + 2 * g + at]
                )
            )
    local.append(pltpu.make_async_copy(len_hbm, len_ref, local_sem.at[11]))
    fetch = pltpu.make_async_copy(q_hbm, q_ref, local_sem.at[12])
    fetch.start()
    pl.semaphore_wait(barrier, len(around))

    for group in ((1, 3), (2,)):
        for d in group:
            to = (x + d) % 4
            send(k_hbm.at[:, lanes(to)], kbuf.at[d], k_ss.at[d], k_rs.at[d], dev(x_=to))
        for d in group:
            to = (x + d) % 4
            send(v_hbm.at[:, lanes(to)], vbuf.at[d], v_ss.at[d], v_rs.at[d], dev(x_=to))

    fetch.wait()
    query = q_ref[...].astype(F32)
    ztile[8] = jnp.zeros((8, 128), F32)
    ztile[8, pl.ds(0, 4, stride=2), :] = query[:, 0:128]
    ztile[8, pl.ds(1, 4, stride=2), 0:96] = query[:, 128:224]
    for hops in (4, 3, 2, 1):
        for way in (hops, -hops):
            to = dev(z_=(z + 16 + way) % 16)
            send(ztile.at[8], ztile.at[8 - way], r_ss.at[8 - way], r_rs.at[8 - way], to)
    for copy in local:
        copy.start()

    local[2].wait()
    wp[:, 224:256, :] = jnp.zeros((16, 32, 256), BF16)
    lane = iota((224, 128), 1)

    def relay(q, carry):
        for r in range(4):
            first, off = (224 * r) // 128, (224 * r) % 128
            tiles = []
            for n in range(3):
                if n < 2 or off >= 64:
                    at = pl.multiple_of(q * 896 + (first + n) * 128, 128)
                    tile = wraw[:, pl.ds(at, 128)].astype(F32)
                    tiles.append(pltpu.roll(tile, 128 - off, 1) if off else tile)
                else:
                    tiles.append(jnp.zeros((224, 128), F32))
            for n in range(2):
                block = jnp.where(lane < 128 - off, tiles[n], tiles[n + 1])
                wp[q * 4 + r, 0:224, n * 128 : (n + 1) * 128] = block.astype(BF16)
        return carry

    lax.fori_loop(0, 4, relay, 0)

    offset = (224 * (2 * yh + c)) % 128
    at, feature = iota((128, 256), 0), iota((128, 256), 1)
    head = 96 + ((feature + offset) >> 7)
    chosen = ((at == head) | (at == head + 16)) & (feature < 224)
    selector[...] = jnp.where(chosen, 1.0, 0.0).astype(BF16)

    mine = yl * 4 + 2 * yh + c

    def pass_on(p):
        @pl.when((p >= 4) & (p != 8) & (p <= 12))
        def _():
            arrived(ztile.at[p], r_rs.at[p])

        def forward(to_p, way):
            pltpu.make_async_remote_copy(
                src_ref=ztile.at[p], dst_ref=ztile.at[to_p], send_sem=f_ss, recv_sem=r_rs.at[to_p],
                device_id=dev(z_=(z + 16 + way) % 16), device_id_type=MESH,
            ).start()

        @pl.when((p >= 4) & (p <= 7))
        def _():
            forward(p - 4, 4)

        @pl.when((p >= 9) & (p <= 11))
        def _():
            forward(p + 4, -4)

    def slot_of(zs):
        return (zs - z + 24) % 16

    for zs in range(16):
        pass_on(slot_of(zs))
    for half in range(2):
        for zs in range(8 * half, 8 * half + 8):
            p = slot_of(zs)

            @pl.when((p < 4) | (p > 12))
            def _():
                arrived(ztile.at[p], r_rs.at[p])

        rows = pl.ds(64 * half, 64)
        for zs in range(8 * half, 8 * half + 8):
            xf[0, 8 * zs : 8 * zs + 8, :] = ztile[slot_of(zs)]
        packed = xf[0, rows, :].astype(BF16)
        qall[mine, rows, :] = packed
        qsend[rows, :] = packed
        for at, (dy, dc) in enumerate(partners):
            send(
                qsend.at[rows], qall.at[mine, rows], qa_ss.at[half, at], qa_rs.at[half, mine],
                dev(y_=(y + dy) % 4, c_=(c + dc) % 2),
            )

    def by_head(half):
        for dy, dc in partners:
            source = (y + dy) % 4
            source = (source % 2) * 4 + (source // 2) * 2 + (c + dc) % 2
            arrived(qall.at[source, pl.ds(64 * half, 64)], qa_rs.at[half, source])
        lane = iota((32, 128), 1)
        xf[:, 64 * half : 64 * half + 64, :] = qall[:, 64 * half : 64 * half + 64, :].astype(F32)
        for side in range(2):
            pieces = [xf[side * 4 + n // 2, pl.ds(64 * half + n % 2, 32, stride=2), :] for n in range(8)]
            starts = [224 * (n // 2) + 128 * (n % 2) for n in range(8)]
            sizes = [128 if n % 2 == 0 else 96 for n in range(8)]
            for h in range(7):
                head = None
                for n in range(8):
                    low = max(starts[n], 128 * h)
                    high = min(starts[n] + sizes[n], 128 * h + 128)
                    if low < high:
                        shift = (starts[n] - 128 * h) % 128
                        moved = pltpu.roll(pieces[n], shift, 1) if shift else pieces[n]
                        if head is None:
                            head = moved
                        else:
                            head = jnp.where(lane < low - 128 * h, head, moved)
                if h <= 3:
                    qf[half, side * 2, h * 32 : (h + 1) * 32, :] = head
                if h >= 3:
                    qf[half, side * 2 + 1, (h - 3) * 32 : (h - 2) * 32, :] = head

    def attend(half, chunks, old_top):
        rows = qf[half, 0:4].reshape(512, 128).astype(BF16)
        top = None
        for n, k in enumerate(chunks):
            scores = lax.dot_general(rows, kbuf[k], ROW_DIMS, preferred_element_type=F32)
            s_ref[:, n * 512 : (n + 1) * 512] = scores
            for m in range(4):
                part = scores[:, m * 128 : (m + 1) * 128]
                top = part if top is None else jnp.maximum(top, part)
        top = (jnp.max(top, axis=1, keepdims=True) * SCALE).astype(BF16).astype(F32)
        top = jnp.broadcast_to(top, (512, 128))
        if old_top is not None:
            top = jnp.maximum(top, old_top)
        total, values = 0.0, 0.0
        for n, k in enumerate(chunks):
            probs = []
            for m in range(4):
                at = n * 512 + m * 128
                part = jnp.exp2(s_ref[:, at : at + 128] * SCALE - top)
                total = total + part
                probs.append(part.astype(BF16))
            probs = jnp.concatenate(probs, axis=1)
            values = values + jnp.dot(probs, vbuf[k], preferred_element_type=F32)
        return top, jnp.broadcast_to(jnp.sum(total, axis=1, keepdims=True), (512, 128)), values

    def keep(top, total, values):
        acc[...] = values.reshape(4, 128, 128)
        tops[...] = top.reshape(4, 128, 128)
        totals[...] = total.reshape(4, 128, 128)

    def to_owners(half):
        lane = iota((32, 128), 1)
        for n in range(4):
            to_y, to_yh = 2 * (n % 2) + n // 2, n % 2
            dy = (to_y - y + 4) % 4
            for to_c in range(2):
                start = 64 * to_yh + 224 * to_c
                off = start % 128
                js = [min(start // 128 + i, 3) for i in range(3)]
                picked = [[part[n, 32 * j : 32 * j + 32, :] for j in js] for part in (acc, tops, totals)]
                moved = [pltpu.roll(part, 128 - off, 1) if off else part for part in picked[0]]
                first = jnp.where(lane < 128 - off, moved[0], moved[1])
                osend[half, n, to_c, 0:32, :] = first.astype(BF16)
                second = jnp.where(lane < 128 - off, moved[1], moved[2])
                second = jnp.where(lane < 96, second, stats(picked[1], picked[2], True))
                osend[half, n, to_c, 32:64, :] = second.astype(BF16)
                here = (dy == 0) & (c == to_c)

                @pl.when(jnp.logical_not(here))
                def _():
                    pltpu.make_async_remote_copy(
                        src_ref=osend.at[half, n, to_c], dst_ref=orecv.at[half, dy * 2 + c], send_sem=o_ss.at[half],
                        recv_sem=o_rs.at[half, dy * 2 + c], device_id=dev(y_=to_y, c_=to_c), device_id_type=MESH,
                    ).start()

                @pl.when(here)
                def _():
                    orecv[half, c] = osend[half, n, to_c]

    lane = iota((1, 128), 1)
    is_top = (lane >= 96) & (lane < 99)
    own_tile = pl.ds(pl.multiple_of(8 * z, 8), 8)

    def merge_partners(half):
        for dy in (2, 1, 3):
            for from_c in range(2):
                arrived(orecv.at[half, dy * 2 + from_c], o_rs.at[half, dy * 2 + from_c])
        arrived(orecv.at[half, 1 - c], o_rs.at[half, 1 - c])
        firsts = [orecv[half, k, 0:32, :].astype(F32) for k in range(8)]
        seconds = [orecv[half, k, 32:64, :].astype(F32) for k in range(8)]
        top = seconds[0]
        for k in range(1, 8):
            top = jnp.maximum(top, seconds[k])
        weight = [jnp.where(is_top, jnp.exp2(part - top), 0.0) for part in seconds]
        wide = spread(jnp.concatenate(weight, axis=0), selector[...])
        first, second, total = 0.0, 0.0, 0.0
        for k in range(8):
            total = total + weight[k] * (pltpu.roll(seconds[k], 124, 1) + pltpu.roll(seconds[k], 120, 1))
            first = first + wide[0][32 * k : 32 * k + 32] * firsts[k]
            second = second + wide[1][32 * k : 32 * k + 32] * seconds[k]
        second = second + jnp.where(is_top, top, 0.0) + pltpu.roll(total, 4, 1)
        zsend[pl.ds(64 * half, 32, stride=2), :] = first
        zsend[pl.ds(64 * half + 1, 32, stride=2), :] = second
        for zs in range(8 * half, 8 * half + 8):

            @pl.when(z != zs)
            def _():
                pltpu.make_async_remote_copy(
                    src_ref=zsend.at[pl.ds(8 * zs, 8)], dst_ref=zrecv.at[own_tile], send_sem=z_ss, recv_sem=z_rs.at[z],
                    device_id=dev(z_=zs), device_id_type=MESH,
                ).start()

    local[0].wait()
    local[1].wait()
    for copy in local[3:]:
        copy.wait()
    for d in (1, 3):
        arrived(kbuf.at[d], k_rs.at[d])
        arrived(vbuf.at[d], v_rs.at[d])

    def send_suffix(dx, to_yh, to_c):
        to_x, slot = (x + dx) % 4, dx * 4 + (yh + to_yh) % 2 * 2 + (c + to_c) % 2
        to_yh, to_c = (yh + to_yh) % 2, (c + to_c) % 2
        send(
            sbuf.at[to_x, 2 * to_yh + to_c], sfx.at[gx], s_ss.at[slot], s_rs.at[gx],
            (to_x * 4 + 2 * to_yh + to_c, gy),
        )

    sfx[gx] = sbuf[x, 2 * yh + c]
    for dx in (1, 3, 0):
        for to_yh in range(2):
            for to_c in range(2):
                if dx or to_yh or to_c:
                    send_suffix(dx, to_yh, to_c)

    by_head(0)
    keep(*attend(0, (0, 1, 3), None))
    arrived(kbuf.at[2], k_rs.at[2])
    arrived(vbuf.at[2], v_rs.at[2])
    old_top = tops[...].reshape(512, 128)
    top, total, values = attend(0, (2,), old_top)
    scale = jnp.exp2(old_top - top)
    keep(
        top, total + scale * totals[...].reshape(512, 128), values + scale * acc[...].reshape(512, 128)
    )
    to_owners(0)

    for to_yh in range(2):
        for to_c in range(2):
            send_suffix(2, to_yh, to_c)

    by_head(1)
    keep(*attend(1, (0, 1, 2, 3), None))
    to_owners(1)

    merge_partners(0)

    for d in range(1, 16):
        source = (gx + d) % 16
        arrived(sfx.at[source], s_rs.at[source])
    mine = 2 * yh + c
    own = [qf[z // 8, yl * 2 + n, pl.ds((z % 8) * 4 + mine, 4, stride=32), :] for n in range(2)]
    own = jnp.concatenate(own, axis=0).astype(BF16)
    suffix_keys = sfx[:, 0].reshape(256, 128)
    suffix_values = sfx[:, 1].reshape(256, 128)
    scores = lax.dot_general(own, suffix_keys, ROW_DIMS, preferred_element_type=F32) * SCALE
    live = iota((8, 256), 1) < len_ref[mine]
    scores = jnp.where(live, scores, -1e30)
    top = jnp.max(scores, axis=1, keepdims=True)
    probs = jnp.where(live, jnp.exp2(scores - top), 0.0)
    total = jnp.sum(probs, axis=1, keepdims=True)
    values = jnp.dot(probs.astype(BF16), suffix_values, preferred_element_type=F32)
    for to in range(4):
        start = 64 * (to // 2) + 224 * (to % 2)
        off = start % 128
        picked = []
        for part in (values, top, total):
            rows = [4 * (to // 2) + min(start // 128 + i, 3) for i in range(3)]
            picked.append([part[row : row + 1] for row in rows])
        moved = [pltpu.roll(part, 128 - off, 1) if off else part for part in picked[0]]
        ssend[to, 0:1, :] = jnp.where(lane < 128 - off, moved[0], moved[1])
        second = jnp.where(lane < 128 - off, moved[1], moved[2])
        ssend[to, 1:2, :] = jnp.where(lane < 96, second, stats(picked[1], picked[2], False))
    near_by = ((1, 0), (1, 1), (0, 1))
    for at, (dyh, dc) in enumerate(near_by):
        to_yh, to_c = (yh + dyh) % 2, (c + dc) % 2
        to = dev(y_=(y + 2 * dyh) % 4, c_=to_c)
        send(ssend.at[2 * to_yh + to_c], srecv.at[mine], h_ss.at[at], h_rs.at[mine], to)
    srecv[mine] = ssend[mine]

    merge_partners(1)
    zrecv[own_tile, :] = zsend[own_tile, :]
    for dyh, dc in near_by:
        source = 2 * ((yh + dyh) % 2) + (c + dc) % 2
        arrived(srecv.at[source], h_rs.at[source])
    tail = iota((8, 128), 0) < 4
    zeros = jnp.zeros((4, 128), F32)
    suffix_first = jnp.concatenate([srecv[t, 0:1, :] for t in range(4)] + [zeros], axis=0)
    suffix_second = jnp.concatenate([srecv[t, 1:2, :] for t in range(4)] + [zeros], axis=0)
    suffix_second = jnp.where(tail | jnp.logical_not(is_top), suffix_second, -1e30)

    for copy in sent:
        copy.wait_send()
    sent.clear()
    pltpu.make_async_remote_copy(
        src_ref=ztile.at[pl.ds(0, 7)], dst_ref=ztile.at[pl.ds(0, 7)], send_sem=f_ss, recv_sem=r_rs.at[8],
        device_id=dev(c_=1 - c), device_id_type=MESH,
    ).wait_send()

    for half in range(2):
        pltpu.make_async_remote_copy(
            src_ref=orecv.at[half, pl.ds(0, 7)], dst_ref=orecv.at[half, pl.ds(0, 7)], send_sem=o_ss.at[half],
            recv_sem=o_rs.at[half, 0], device_id=dev(c_=1 - c), device_id_type=MESH,
        ).wait_send()

    for hops in range(1, 16):
        source = (z + hops) % 16
        arrived(zrecv.at[pl.ds(pl.multiple_of(8 * source, 8), 8)], z_rs.at[source])
    first = zrecv[pl.ds(0, 64, stride=2), :]
    second = zrecv[pl.ds(1, 64, stride=2), :]
    firsts = [first[8 * k : 8 * k + 8] for k in range(8)] + [suffix_first]
    seconds = [second[8 * k : 8 * k + 8] for k in range(8)] + [suffix_second]
    top = seconds[0]
    for k in range(1, 9):
        top = jnp.maximum(top, seconds[k])
    top = jnp.maximum(top, pltpu.roll(top, 4, 0))
    weight = [jnp.where(is_top, jnp.exp2(part - top), 0.0) for part in seconds]
    wide = spread(jnp.concatenate(weight, axis=0), selector[...])
    first, second, total = 0.0, 0.0, 0.0
    for k in range(9):
        first = first + wide[0][8 * k : 8 * k + 8] * firsts[k]
        second = second + wide[1][8 * k : 8 * k + 8] * seconds[k]
        total = total + weight[k] * pltpu.roll(seconds[k], 124, 1)
    first = first + pltpu.roll(first, 4, 0)
    second = second + pltpu.roll(second, 4, 0)
    total = total + pltpu.roll(total, 4, 0)
    wide = spread(total, selector[...])
    second = jnp.where(lane < 96, second / wide[1], 0.0)
    features = jnp.concatenate([first / wide[0], second], axis=1).astype(BF16)

    row = iota((8, 128), 0)
    others = [(dx, dyh, dc) for dx in range(4) for dyh in range(2) for dc in range(2)]
    others.sort(key=lambda move: -(min(move[0], 4 - move[0]) + 2 * move[1] + move[2]))
    for at, (dx, dyh, dc) in enumerate(others):
        to = ((x + dx) % 4) * 4 + ((yh + dyh) % 2) * 2 + (c + dc) % 2
        product = jnp.dot(features, wp[to], preferred_element_type=F32)
        tile = jnp.where(row < 4, product[:, 0:128], product[:, 128:256])
        if at < 15:
            psend[at] = tile
            send(psend.at[at], precv.at[at], p_ss.at[at], p_rs.at[at], (to, gy))
    for at in range(15):
        arrived(precv.at[at], p_rs.at[at])
    for at in range(15):
        tile = tile + precv[at]
    pltpu.make_async_remote_copy(
        src_ref=zsend.at[pl.ds(0, 120)], dst_ref=zsend.at[pl.ds(0, 120)], send_sem=z_ss, recv_sem=z_rs.at[0],
        device_id=dev(c_=1 - c), device_id_type=MESH,
    ).wait_send()
    result = tile
    o_ref[:, 0:128] = result[0:4].astype(BF16)
    o_ref[:, 128:224] = result[4:8, 0:96].astype(BF16)
    for copy in sent:
        copy.wait_send()


def on_device(query, keys, values, suffix_keys, suffix_values, lengths, out_weight):
    hbm = pl.BlockSpec(memory_space=pltpu.HBM)
    dma = pltpu.SemaphoreType.DMA
    return pl.pallas_call(
        kernel,
        out_shape=jax.ShapeDtypeStruct((4, 224), BF16),
        in_specs=[hbm] * 7,
        out_specs=pl.BlockSpec(memory_space=pltpu.VMEM),
        scratch_shapes=[
            pltpu.VMEM((4, 224), BF16),
            pltpu.SMEM((4,), jnp.int32),
            pltpu.VMEM((4, 512, 128), BF16),
            pltpu.VMEM((4, 512, 128), BF16),
            pltpu.VMEM((224, 3584), BF16),
            pltpu.VMEM((16, 256, 256), BF16),
            pltpu.VMEM((4, 4, 2, 16, 128), BF16),
            pltpu.VMEM((16, 2, 16, 128), BF16),
            pltpu.VMEM((16, 8, 128), F32),
            pltpu.VMEM((128, 128), BF16),
            pltpu.VMEM((8, 128, 128), BF16),
            pltpu.VMEM((8, 128, 128), F32),
            pltpu.VMEM((2, 6, 128, 128), F32),
            pltpu.VMEM((512, 2048), F32),
            pltpu.VMEM((4, 128, 128), F32),
            pltpu.VMEM((4, 128, 128), F32),
            pltpu.VMEM((4, 128, 128), F32),
            pltpu.VMEM((128, 256), BF16),
            pltpu.VMEM((2, 4, 2, 64, 128), BF16),
            pltpu.VMEM((2, 8, 64, 128), BF16),
            pltpu.VMEM((144, 128), F32),
            pltpu.VMEM((144, 128), F32),
            pltpu.VMEM((4, 8, 128), F32),
            pltpu.VMEM((4, 8, 128), F32),
            pltpu.VMEM((16, 8, 128), F32),
            pltpu.VMEM((16, 8, 128), F32),
            dma((13,)),
            dma((4,)), dma((4,)), dma((4,)), dma((4,)),
            dma((16,)), dma((16,)),
            dma((16,)), dma((16,)), dma,
            dma((2, 7)), dma((2, 8)),
            dma((2,)), dma((2, 8)),
            dma, dma((16,)),
            dma((3,)), dma((4,)),
            dma((16,)), dma((16,)),
        ],
        compiler_params=pltpu.CompilerParams(
            collective_id=0, has_side_effects=True, vmem_limit_bytes=56 * 2**20
        ),
        name="decode_attention",
    )(query, keys, values, suffix_keys, suffix_values, lengths, out_weight)


def solution(mesh):
    return jax.shard_map(
        on_device,
        mesh=mesh,
        in_specs=(
            P("gy", "gx"),
            P(("gx", "gy"), None),
            P(("gx", "gy"), None),
            P("gy", "gx", None),
            P("gy", "gx", None),
            P("gy"),
            P("gx", None),
        ),
        out_specs=P("gy", "gx"),
        check_vma=False,
    )
```
